256 devices in a mesh: section: 8 (over y, core), expert: 32 (over x, z).
Axes of the slice: x: 4, y: 4, z: 8, core: 2. Of those that a mesh axis runs over, the one named last changes fastest.
Arguments:
- inputs: bfloat16 [8, 512, 768], P('section', None, 'expert'), may hold values from -6 to 6
- routes: int32 [2, 8, 8, 512, 2], P(None, 'section'), may hold values from 0 to 31, all different within a row; in each aligned block of 512 rows (0 to 511, 512 to 1023, ..., all dimensions but the last counted through in order) at most 48 rows name the same one
- norm_gains: bfloat16 [2, 8, 768], P(None, 'section'), may hold values from 0.25 to 1.75
- routers: bfloat16 [2, 8, 32, 768], P(None, 'section', 'expert'), may hold values from -0.21875 to 0.21875
- expert_in: bfloat16 [2, 8, 32, 1536, 768], P(None, 'section', 'expert'), may hold values from -0.21875 to 0.21875
- expert_out: bfloat16 [2, 8, 32, 1536, 768], P(None, 'section', 'expert'), may hold values from -0.15625 to 0.15625
Outputs:
- outputs: bfloat16 [8, 512, 768], P('section', None, 'expert')
The draws below stay inside these ranges and needn't reach their ends.
Inputs may be any that keep to these rules, and one draw needn't show every extreme that they name: `routes`: in each layer and micro-batch no expert is named by more than 48 tokens; a token's two ids differ.
All inputs are finite; a program needn't handle non-finite values.
Results may differ from the reference program's by a relative error of at most 0.034.
Values may be sent and summed in bfloat16 or wider, within the bound.
No kernel may reach another device: no remote copies, remote signals or barrier semaphores. Data moves between devices by JAX's collectives and lax.ppermute only.
A program may use at most 64 MiB of HBM per device.

```python
import math
import jax
import jax.numpy as jnp
import numpy as np
from jax import lax

D = 768
FF_WIN = 1536
EXPERTS = 32
REPEATS = 2
MB_TOKENS = 512
MICRO = 8
CAP = 48
N_SECTION = 8


def steps_of(rng, dims, shards, low, high):
    factor_of, own = 1.0, jax.random.fold_in(rng, 6)
    for axis_at, shards_of in shards:
        heights = jnp.exp(jax.random.uniform(jax.random.fold_in(own, axis_at), (shards_of,), jnp.float32, low / len(shards), high / len(shards)))
        factor_of = factor_of * jnp.repeat(heights, dims[axis_at] // shards_of).reshape([-1 if axis == axis_at else 1 for axis in range(len(dims))])
    return factor_of


def assign_block(own_key, own, number, rows, count, top, reach, skew):
    ranking = jax.random.permutation(own_key, count)
    heavy_load, usual = load_shares(count, rows * top, reach, skew, True), load_shares(count, rows * top, reach, skew, False)
    places = jnp.arange(count)

    def named(tallies, offset_by):
        used = int((tallies > 0).sum())
        fixed = max(1, used // 4)
        moved = fixed + (places - fixed + offset_by * (used - fixed)) % max(1, count - fixed)
        return jnp.zeros((count,), jnp.int32).at[ranking[jnp.where(places < fixed, places, moved)]].set(jnp.asarray(tallies, jnp.int32))

    tallies = jnp.where(number % 4 == 0, named(heavy_load, number // 4), named(usual, number - number // 4 - 1))
    mixed = jax.random.permutation(jax.random.fold_in(own, 3), count)
    giver, receiver = mixed[0:count // 2 * 2:2], mixed[1:count // 2 * 2:2]
    room = jnp.minimum(tallies[giver] - 1, reach - tallies[receiver]) // 2
    room = jnp.where((giver == ranking[0]) | (receiver == ranking[0]) | (tallies[receiver] == 0), 0, jnp.maximum(room, 0))
    moved = jax.random.randint(jax.random.fold_in(own, 4), (count // 2,), 0, 1 << 20) % (room + 1)
    tallies = tallies.at[giver].add(-moved).at[receiver].add(moved)
    items = jnp.searchsorted(jnp.cumsum(tallies), jnp.arange(rows * top), side="right").astype(jnp.int32)
    table = items.reshape(top, rows).T
    table = table[jax.random.permutation(jax.random.fold_in(own, 1), rows)]
    offset_by = jax.random.randint(jax.random.fold_in(own, 2), (rows, 1), 0, top)
    return jnp.take_along_axis(table, (jnp.arange(top)[None, :] + offset_by) % top, axis=1)


def load_shares(amount, total, reach, slope, full):
    portions = [(1 << 20) // math.isqrt(rank ** slope) + 1 for rank in range(1, amount + 1)]
    largest = reach if full else min(reach, max(-(-total // amount), total * portions[0] // sum(portions)))
    least = 1 if total - largest >= amount - 1 else 0
    holding, surplus = [largest] + [least] * (amount - 1), total - largest - least * (amount - 1)
    while surplus > 0:
        movable = [i for i in range(1, amount) if holding[i] < largest] or [i for i in range(1, amount) if holding[i] < reach]
        whole, left = sum([portions[i] for i in movable]), surplus
        for i in movable:
            extra = min(reach - holding[i], max(1, left * portions[i] // whole), surplus)
            holding[i] = holding[i] + extra
            surplus = surplus - extra
    return np.array(holding)


def gaussian(stream_key, extent, deviation, limit, cuts=(), held_as=jnp.bfloat16):
    gain = steps_of(stream_key, extent, cuts, -0.22, 0.18) if cuts else 1.0
    values = jax.random.normal(stream_key, extent, jnp.float32) * deviation * gain
    return jnp.minimum(jnp.maximum(values, -limit), limit).astype(held_as)


def setup_inputs(seed: int = 0) -> dict:
    seeds = jax.random.split(jax.random.key(seed), 7)
    inputs = gaussian(seeds[0], (MICRO, MB_TOKENS, D), 1.0, 6.0, ((0, 8), (2, 32)))
    routes_keys = jax.random.split(jax.random.fold_in(seeds[1], 1), REPEATS * N_SECTION * MICRO * MB_TOKENS // MB_TOKENS)
    routes_turns = jax.random.permutation(jax.random.fold_in(seeds[1], 3), REPEATS * N_SECTION * MICRO * MB_TOKENS // MB_TOKENS)
    routes = jax.vmap(lambda own, number: assign_block(jax.random.fold_in(seeds[1], 2), own, number, MB_TOKENS, EXPERTS, 2, CAP, 2))(routes_keys, routes_turns).reshape((REPEATS, N_SECTION, MICRO, MB_TOKENS, 2))
    norm_gains = jnp.clip(1.0 + 0.15 * jax.random.normal(seeds[2], (REPEATS, N_SECTION, D), jnp.float32), 0.25, 1.75).astype(jnp.bfloat16)
    routers = gaussian(seeds[3], (REPEATS, N_SECTION, EXPERTS, D), D ** -0.5, 0.21875, ((1, 8), (2, 32)))
    expert_in = gaussian(seeds[4], (REPEATS, N_SECTION, EXPERTS, FF_WIN, D), D ** -0.5, 0.21875, ((1, 8), (2, 32)))
    expert_out = gaussian(seeds[5], (REPEATS, N_SECTION, EXPERTS, FF_WIN, D), FF_WIN ** -0.5, 0.15625, ((1, 8), (2, 32)))
    return {"inputs": inputs, "routes": routes, "norm_gains": norm_gains, "routers": routers, "expert_in": expert_in, "expert_out": expert_out}


def place_rows(chosen, experts, capacity):
    flat_ids = chosen.reshape(-1).astype(jnp.int32)
    onehot = (flat_ids[:, None] == jnp.arange(experts, dtype=jnp.int32)[None, :]).astype(jnp.int32)
    rank_table = (jnp.cumsum(onehot, axis=0) - 1).astype(jnp.int32)
    slot_ids = lax.optimization_barrier(jnp.sum(rank_table * onehot, axis=1)).astype(jnp.int32)
    owners = (jnp.arange(flat_ids.shape[0], dtype=jnp.int32) // 2).astype(jnp.int32)
    slot_table = jnp.full((experts * capacity,), -1, jnp.int32).at[flat_ids * capacity + slot_ids].set(owners)
    return (slot_table.reshape(experts, capacity), flat_ids, slot_ids)

def combine(current, returned, gate_grid, flat_ids, slot_ids, experts):
    flat_index = slot_ids * experts + flat_ids
    picked_vals = returned.reshape(-1, returned.shape[2])[flat_index].astype(jnp.float32)
    weights = gate_grid.reshape(-1)[flat_index].astype(jnp.float32)
    branch_sum = picked_vals.reshape(-1, 2, picked_vals.shape[1]).sum(axis=1)
    gate_sum = weights.reshape(-1, 2).sum(axis=1)
    return (current.astype(jnp.float32) + branch_sum / gate_sum[:, None]).astype(jnp.bfloat16)

def mix_layer(current, chosen, gain_row, router_rows, weight_in, weight_out):
    slot_table, flat_ids, slot_ids = place_rows(chosen, EXPERTS, CAP)
    row_block = jnp.take(current, jnp.maximum(slot_table, 0), axis=0)
    row_block = jnp.where((slot_table >= 0)[:, :, None], row_block, jnp.zeros_like(row_block))
    widened = row_block.astype(jnp.float32)
    mean_square = lax.optimization_barrier(jnp.mean(widened * widened, axis=2, keepdims=True))
    normed = (widened * lax.rsqrt(mean_square + 1e-06) * gain_row.astype(jnp.float32)).astype(jnp.bfloat16)
    pre_act = jnp.einsum('ecd,ehd->ech', normed.astype(jnp.float32), weight_in.astype(jnp.float32))
    active = jax.nn.gelu(pre_act).astype(jnp.bfloat16)
    output = jnp.einsum('ech,ehd->ecd', active.astype(jnp.float32), weight_out.astype(jnp.float32))
    logit_value = jnp.einsum('ecd,ed->ec', normed.astype(jnp.float32), router_rows.astype(jnp.float32))
    gate_value = jax.nn.sigmoid(logit_value).astype(jnp.bfloat16)
    weighted = (output * gate_value.astype(jnp.float32)[:, :, None]).astype(jnp.bfloat16)
    returned = jnp.transpose(weighted, (1, 0, 2))
    gate_grid = jnp.transpose(gate_value, (1, 0))
    return combine(current, returned, gate_grid, flat_ids, slot_ids, EXPERTS)

def reference(inputs, routes, norm_gains, routers, expert_in, expert_out):

    def one_micro(pair):
        micro_in, micro_routes = pair

        def layer_step(layer_id, current):
            repeat_id = layer_id // N_SECTION
            section_id = layer_id % N_SECTION
            return mix_layer(current, micro_routes[repeat_id, section_id], norm_gains[repeat_id, section_id], routers[repeat_id, section_id], expert_in[repeat_id, section_id], expert_out[repeat_id, section_id])
        return lax.fori_loop(0, REPEATS * N_SECTION, layer_step, micro_in)
    return lax.map(one_micro, (inputs, jnp.moveaxis(routes, 2, 0)))
```

```python
import functools

import jax
import jax.numpy as jnp
import numpy as np
from jax import lax
from jax.experimental import pallas as pl
from jax.experimental.pallas import tpu as pltpu
from jax.sharding import PartitionSpec as P

VMEM_LIMIT = 62 * 1024 * 1024
HBM = pl.BlockSpec(memory_space=pltpu.HBM)
SMEM = pl.BlockSpec(memory_space=pltpu.SMEM)
VMEM = pl.BlockSpec(memory_space=pltpu.VMEM)
DIRS = (1, -1)


def owner_of(layer, sections):
    return (layer % sections) // 2


def ring_plan(sections, layers):
    chips = sections // 2
    held = [
        [{q: 0 for q in range(layers) if owner_of(q, sections) == y} for y in range(chips)]
        for _ in DIRS
    ]
    slots = []
    while any(len(stock) < layers for lane in held for stock in lane):
        moves = []
        for lane, step in enumerate(DIRS):
            for y in range(chips):
                there = held[lane][(y + step) % chips]
                options = [q for q in held[lane][y] if q not in there]
                if options:
                    moves.append((lane, y, (y + step) % chips, min(options)))
        slots.append(moves)
        for lane, y, target, q in moves:
            held[lane][target][q] = len(slots)
    return slots, held


def pick_kernel(row, places, tab_ref, *refs):
    count = len(places)
    sources, out_ref, sem = refs[:count], refs[count], refs[count + 1]
    choice = tab_ref[row]
    for number, (source, place) in enumerate(zip(sources, places)):
        view = source.at[place] if place else source

        @pl.when(choice == number)
        def _(view=view):
            copy = pltpu.make_async_copy(view, out_ref, sem)
            copy.start()
            copy.wait()


def pick(tab, row, sources, places):
    shape = sources[0].shape[-2:]
    size = 2 * shape[0] * shape[1] * 2
    return pl.pallas_call(
        functools.partial(pick_kernel, row, places),
        out_shape=jax.ShapeDtypeStruct(shape, jnp.bfloat16),
        in_specs=[SMEM] + [HBM] * len(sources),
        out_specs=HBM,
        scratch_shapes=[pltpu.SemaphoreType.DMA],
        compiler_params=pltpu.CompilerParams(vmem_limit_bytes=VMEM_LIMIT),
        cost_estimate=pl.CostEstimate(flops=0, bytes_accessed=size, transcendentals=0),
        name="pick",
    )(tab, *sources)


def merge_rows(h_ref, gathered_ref, scale_ref, col_ref, start, size):
    rows = pl.ds(start, size)
    slots = gathered_ref.shape[0]
    lanes = lax.broadcasted_iota(jnp.int32, (size, slots), 1)
    first, second = col_ref[rows, 0:1], col_ref[rows, 1:2]
    onehot = jnp.where((lanes == first) | (lanes == second), 1.0, 0.0).astype(jnp.bfloat16)
    update = jnp.dot(onehot, gathered_ref[...], preferred_element_type=jnp.float32)
    return (h_ref[rows, :].astype(jnp.float32) + update * scale_ref[rows, :]).astype(jnp.bfloat16)


def layer_kernel(
    merge, block, scal_ref, h_ref, gathered_ref, scale_ref, colp_ref, col_ref, row_ref,
    router_ref, gain_ref, lane_ref, other_ref, hnew_ref, weighted_ref, newscale_ref,
    win_ref, wout_ref, normed_ref, gates_ref, sems,
):
    core, expert = scal_ref[0], scal_ref[1]

    @pl.when(core == 0)
    def _():
        pltpu.make_async_copy(lane_ref, win_ref, sems.at[0]).start()
        pltpu.make_async_copy(other_ref, wout_ref, sems.at[1]).start()

    @pl.when(core != 0)
    def _():
        pltpu.make_async_copy(other_ref, win_ref, sems.at[0]).start()
        pltpu.make_async_copy(lane_ref, wout_ref, sems.at[1]).start()

    tokens = h_ref.shape[0]
    experts = router_ref.shape[0]
    capacity = weighted_ref.shape[0]
    gain = gain_ref[...]
    ids = lax.broadcasted_iota(jnp.int32, (block, experts), 1)
    @pl.loop(0, tokens // block)
    def _(turn):
        start = pl.multiple_of(turn * block, block)
        rows = pl.ds(start, block)
        if merge:
            held = merge_rows(h_ref, gathered_ref, scale_ref, colp_ref, start, block)
            hnew_ref[rows, :] = held
        else:
            held = h_ref[rows, :]
            hnew_ref[rows, :] = held
        wide = held.astype(jnp.float32)
        mean_square = jnp.mean(wide * wide, axis=1, keepdims=True)
        normed = (wide * lax.rsqrt(mean_square + 1e-06) * gain).astype(jnp.bfloat16)
        normed_ref[rows, :] = normed
        logits = lax.dot_general(
            normed, router_ref[...], (((1,), (1,)), ((), ())), preferred_element_type=jnp.float32
        )
        gates = jax.nn.sigmoid(logits).astype(jnp.bfloat16)
        gates_ref[rows, :] = gates
        named = (ids == col_ref[rows, 2:3]) | (ids == col_ref[rows, 3:4])
        total = jnp.sum(jnp.where(named, gates.astype(jnp.float32), 0.0), axis=1, keepdims=True)
        newscale_ref[rows, :] = 1.0 / total

    slots = lax.broadcasted_iota(jnp.int32, (capacity, tokens), 0) + expert * capacity
    chosen = (slots == row_ref[0:1, :]) | (slots == row_ref[1:2, :])
    chosen = jnp.where(chosen, 1.0, 0.0).astype(jnp.bfloat16)
    taken = jnp.dot(chosen, normed_ref[...], preferred_element_type=jnp.float32)
    taken = taken.astype(jnp.bfloat16)
    all_gates = jnp.dot(chosen, gates_ref[...], preferred_element_type=jnp.float32)
    own = lax.broadcasted_iota(jnp.int32, all_gates.shape, 1) == expert
    gate = jnp.sum(jnp.where(own, all_gates, 0.0), axis=1, keepdims=True)
    pltpu.make_async_copy(lane_ref, win_ref, sems.at[0]).wait()
    pre_act = lax.dot_general(
        taken, win_ref[...], (((1,), (1,)), ((), ())), preferred_element_type=jnp.float32
    )
    active = jax.nn.gelu(pre_act, approximate=True).astype(jnp.bfloat16)
    pltpu.make_async_copy(lane_ref, wout_ref, sems.at[1]).wait()
    output = jnp.dot(active, wout_ref[...], preferred_element_type=jnp.float32)
    weighted_ref[...] = (output * gate).astype(jnp.bfloat16)


def plane(shape, *lead):
    return pl.BlockSpec((None,) * len(lead) + shape, lambda i: lead + (0,) * len(shape))


def run_layer(layer, scal, h, gathered, scale, cols, rows, routers, gains, lane_w, other_w):
    tokens, width = h.shape
    hidden = lane_w.shape[0]
    experts = routers.shape[1]
    capacity = 3 * tokens // experts
    merge = layer > 0
    before = max(layer - 1, 0)
    operands = (scal, h, gathered, scale, cols, cols, rows, routers, gains, lane_w, other_w)
    flops = 4 * capacity * hidden * width + 2 * tokens * experts * capacity * width
    return pl.pallas_call(
        functools.partial(layer_kernel, merge, min(128, tokens)),
        out_shape=(
            jax.ShapeDtypeStruct((tokens, width), jnp.bfloat16),
            jax.ShapeDtypeStruct((capacity, width), jnp.bfloat16),
            jax.ShapeDtypeStruct((tokens, 1), jnp.float32),
        ),
        grid=(1,),
        in_specs=[
            SMEM, VMEM, VMEM, VMEM,
            plane((tokens, 4), before), plane((tokens, 4), layer), plane((8, tokens), layer),
            plane((experts, width), layer), plane((1, width), layer),
            HBM, HBM,
        ],
        out_specs=(VMEM, VMEM, VMEM),
        scratch_shapes=[
            pltpu.VMEM((hidden, width), jnp.bfloat16),
            pltpu.VMEM((hidden, width), jnp.bfloat16),
            pltpu.VMEM((tokens, width), jnp.bfloat16),
            pltpu.VMEM((tokens, experts), jnp.bfloat16),
            pltpu.SemaphoreType.DMA((2,)),
        ],
        compiler_params=pltpu.CompilerParams(vmem_limit_bytes=VMEM_LIMIT),
        cost_estimate=pl.CostEstimate(
            flops=flops, bytes_accessed=4 * hidden * width + 4 * tokens * width, transcendentals=0
        ),
        name="layer",
    )(*operands)


def final_kernel(block, h_ref, gathered_ref, scale_ref, col_ref, out_ref):
    @pl.loop(0, h_ref.shape[0] // block)
    def _(turn):
        start = pl.multiple_of(turn * block, block)
        out_ref[pl.ds(start, block), :] = merge_rows(
            h_ref, gathered_ref, scale_ref, col_ref, start, block
        )


def run_final(last, h, gathered, scale, cols):
    tokens = h.shape[0]
    return pl.pallas_call(
        functools.partial(final_kernel, min(128, tokens)),
        out_shape=jax.ShapeDtypeStruct(h.shape, jnp.bfloat16),
        grid=(1,),
        in_specs=[VMEM, VMEM, VMEM, plane((tokens, 4), last)],
        out_specs=VMEM,
        compiler_params=pltpu.CompilerParams(vmem_limit_bytes=VMEM_LIMIT),
        name="final",
    )(h, gathered, scale, cols)


def place_tokens(routes, experts, capacity):
    layers, tokens, _ = routes.shape
    ids = jnp.arange(experts, dtype=jnp.int32)
    first = routes[:, :, 0:1] == ids
    second = routes[:, :, 1:2] == ids
    named = (first | second).astype(jnp.bfloat16)
    earlier = jnp.tril(jnp.ones((tokens, tokens), jnp.bfloat16), -1)
    rank = jnp.einsum("ut,lte->lue", earlier, named, preferred_element_type=jnp.float32)
    rank = rank.astype(jnp.int32) + ids * capacity
    slot_first = jnp.sum(jnp.where(first, rank, 0), axis=2)
    slot_second = jnp.sum(jnp.where(second, rank, 0), axis=2)
    cols = jnp.stack([slot_first, slot_second, routes[:, :, 0], routes[:, :, 1]], axis=2)
    blank = jnp.zeros_like(slot_first)
    rows = jnp.stack([slot_first, slot_second] + [blank] * 6, axis=1)
    return cols, rows


def local(inputs, routes, norm_gains, routers, expert_in, expert_out):
    sections = lax.axis_size("section")
    experts = lax.axis_size("expert")
    section_pos = lax.axis_index("section")
    expert_pos = lax.axis_index("expert")
    repeats = expert_in.shape[0]
    layers = repeats * sections
    tokens = inputs.shape[1]
    capacity = 3 * tokens // experts
    slots, held = ring_plan(sections, layers)
    arrival = [max(stock[q] for lane in held for stock in lane) for q in range(layers)]
    scal = jnp.stack([section_pos % 2, expert_pos]).astype(jnp.int32)

    def source_of(lane, y, q):
        if owner_of(q, sections) == y:
            if q % 2 == lane:
                return ("in", "out")[lane], q // sections
            return "swapped", q // sections
        return "ring", held[lane][y][q]

    buffers = {("in", r): (expert_in, (r, 0, 0)) for r in range(repeats)}
    buffers.update({("out", r): (expert_out, (r, 0, 0)) for r in range(repeats)})
    table, wanted = [], []

    def add_pick(by_section):
        names = sorted(set(by_section.values()))
        table.append([names.index(by_section[s]) if s in by_section else 0 for s in range(sections)])
        wanted.append(names)
        return len(table) - 1

    every = [(lane, y) for lane in range(2) for y in range(sections // 2)]
    swap_rows = [
        add_pick({2 * y + lane: (("out", "in")[lane], r) for lane, y in every})
        for r in range(repeats)
    ]
    ring_rows = [
        add_pick({2 * y + lane: source_of(lane, y, q) for lane, y, _, q in moves}) for moves in slots
    ]
    layer_rows = [
        add_pick({2 * y + lane: source_of(lane, y, q) for lane, y in every}) for q in range(layers)
    ]
    tab = jnp.asarray(np.array(table, np.int32).T)[section_pos]

    def picked(row, tab):
        found = [buffers[name] for name in wanted[row]]
        return pick(tab, row, [array for array, _ in found], [place for _, place in found])

    def swapped(value):
        return lax.ppermute(value, "section", [(s, s ^ 1) for s in range(sections)])

    def ring(slot, tab):
        pairs = [(2 * y + lane, 2 * target + lane) for lane, y, target, _ in slots[slot]]
        return lax.ppermute(picked(ring_rows[slot], tab), "section", pairs)

    mine = lax.all_to_all(routes[:, 0], "section", split_axis=1, concat_axis=0, tiled=False)
    mine = jnp.transpose(mine, (1, 0, 2, 3)).reshape(layers, tokens, 2)
    cols, rows = place_tokens(mine, experts, capacity)
    gains = lax.all_gather(norm_gains[:, 0], "section", axis=0)
    gains = jnp.transpose(gains, (1, 0, 2)).reshape(layers, 1, -1).astype(jnp.float32)
    gate_rows = lax.all_gather(routers[:, 0, 0], ("section", "expert"), axis=0)
    gate_rows = gate_rows.reshape(sections, experts, repeats, -1)
    gate_rows = jnp.transpose(gate_rows, (2, 0, 1, 3)).reshape(layers, experts, -1)
    h = lax.all_gather(inputs[0], "expert", axis=1, tiled=True)

    buffers[("swapped", 0)] = (swapped(picked(swap_rows[0], tab)), ())
    later = swapped(picked(swap_rows[1], tab))
    lead = arrival[0]
    for slot in range(lead):
        arrived = ring(slot, tab)
        if slot == 0:
            arrived, later, tab = lax.optimization_barrier((arrived, later, tab))
            buffers[("swapped", 1)] = (later, ())
        else:
            arrived, tab = lax.optimization_barrier((arrived, tab))
        buffers[("ring", slot + 1)] = (arrived, ())
    lane_w = picked(layer_rows[0], tab)
    other_w = swapped(lane_w)
    state = lax.optimization_barrier((lane_w, other_w, tab, cols, rows, gains, gate_rows, h))
    lane_w, other_w, tab, cols, rows, gains, gate_rows, h = state
    gathered = jnp.zeros((8, h.shape[1]), jnp.bfloat16)
    scale = jnp.zeros((8, 1), jnp.float32)

    for q in range(layers):
        slot = lead + q
        arrived = ring(slot, tab) if slot < len(slots) else None
        h, weighted, scale = run_layer(
            q, scal, h, gathered, scale, cols, rows, gate_rows, gains, lane_w, other_w
        )
        weighted, tab = lax.optimization_barrier((weighted, tab))
        gathered = lax.all_gather(weighted, "expert", axis=0, tiled=True)
        early = q + 1 < layers and arrival[q + 1] <= slot
        if early:
            lane_w = picked(layer_rows[q + 1], tab)
            other_w = swapped(lane_w)
        if arrived is not None:
            state = lax.optimization_barrier((gathered, arrived, lane_w, other_w, tab))
            gathered, arrived, lane_w, other_w, tab = state
            buffers[("ring", slot + 1)] = (arrived, ())
        else:
            state = lax.optimization_barrier((gathered, lane_w, other_w, tab))
            gathered, lane_w, other_w, tab = state
        if q + 1 < layers and not early:
            lane_w = picked(layer_rows[q + 1], tab)
            other_w = swapped(lane_w)

    h = run_final(layers - 1, h, gathered, scale, cols)
    width = inputs.shape[2]
    return lax.dynamic_slice(h, (0, expert_pos * width), (tokens, width))[None]


def solution(mesh):
    return jax.shard_map(
        local,
        mesh=mesh,
        in_specs=(
            P("section", None, "expert"),
            P(None, "section", None, None, None),
            P(None, "section", None),
            P(None, "section", "expert", None),
            P(None, "section", "expert", None, None),
            P(None, "section", "expert", None, None),
        ),
        out_specs=P("section", None, "expert"),
        check_vma=False,
    )
```

```python
import functools

import jax
import jax.numpy as jnp
import numpy as np
from jax import lax
from jax.experimental import pallas as pl
from jax.experimental.pallas import tpu as pltpu
from jax.sharding import PartitionSpec as P

VMEM_LIMIT = 62 * 1024 * 1024
HBM = pl.BlockSpec(memory_space=pltpu.HBM)
SMEM = pl.BlockSpec(memory_space=pltpu.SMEM)
VMEM = pl.BlockSpec(memory_space=pltpu.VMEM)
DIRS = (1, -1)


PACK = 64
PARTS = 2
LEAD = 7
SKIP = 5


def ring_plan(sections, layers, parts, lead, skip):
    chips = sections // 2
    items = layers * parts
    owned = [[i for i in range(items) if (i // parts) % sections // 2 == y] for y in range(chips)]
    held = [[dict.fromkeys(owned[y], 0) for y in range(chips)] for _ in DIRS]
    phases = []
    while any(len(stock) < items for lane in held for stock in lane):
        number = len(phases) + 1
        moves = []
        for lane, step in enumerate(DIRS):
            for y in range(chips):
                target = (y + step) % chips
                options = [i for i, at in held[lane][y].items() if at < number]
                options = [i for i in options if i not in held[lane][target]]
                if options and not (number >= lead + 8 and (number - lead - 7) % skip == 0):
                    moves.append((lane, y, target, min(options)))
        phases.append(moves)
        for lane, y, target, i in moves:
            held[lane][target][i] = number if number < lead else number + 1
    return phases, held


def pick_kernel(rows, places, tab_ref, *refs):
    count = len(refs) - 4
    sources, out_ref, hold_ref, in_sems, out_sems = refs[:count], *refs[count:]
    size = hold_ref.shape[0] // len(rows)
    step = size // 2

    def copies(part, view):
        for half in range(2):
            to = part * size + half * step
            yield pltpu.make_async_copy(
                view.at[pl.ds(half * step, step)],
                hold_ref.at[pl.ds(to, step)],
                in_sems.at[part * 2 + half],
            )

    def view_of(number, start):
        place = places[number]
        return sources[number].at[place + (pl.ds(start, size),)]

    used = 0
    for part, (row, choices) in enumerate(rows):
        choice = tab_ref[row]
        for number, (source, start) in enumerate(choices):

            @pl.when(choice == number)
            def _(part=part, source=source, start=start):
                for copy in copies(part, view_of(source, start)):
                    copy.start()

    for part, (row, choices) in enumerate(rows):
        for half, copy in enumerate(copies(part, view_of(*choices[0]))):
            copy.wait()
            at = pl.ds(part * size + half * step, step)
            number = part * 2 + half
            pltpu.make_async_copy(hold_ref.at[at], out_ref.at[at], out_sems.at[number]).start()
    for part in range(len(rows)):
        for half in range(2):
            at = pl.ds(part * size + half * step, step)
            number = part * 2 + half
            pltpu.make_async_copy(hold_ref.at[at], out_ref.at[at], out_sems.at[number]).wait()


def pick(tab, rows, sources, places, size, width):
    total = size * len(rows)
    return pl.pallas_call(
        functools.partial(pick_kernel, rows, places),
        out_shape=jax.ShapeDtypeStruct((total, width), jnp.bfloat16),
        in_specs=[SMEM] + [HBM] * len(sources),
        out_specs=HBM,
        scratch_shapes=[
            pltpu.VMEM((total, width), jnp.bfloat16),
            pltpu.SemaphoreType.DMA((2 * len(rows),)),
            pltpu.SemaphoreType.DMA((2 * len(rows),)),
        ],
        compiler_params=pltpu.CompilerParams(vmem_limit_bytes=VMEM_LIMIT),
        cost_estimate=pl.CostEstimate(
            flops=0, bytes_accessed=4 * total * width, transcendentals=0
        ),
        name="pick",
    )(tab, *sources)


def unpack_pairs(back):
    low = lax.broadcasted_iota(jnp.int32, (1, 1, 2 * PACK), 2) < PACK
    pairs = back.shape[0] // 2
    split = back.reshape(pairs, 2, 16, 2 * PACK)
    even, odd = split[:, 0], split[:, 1]
    turned_even = pltpu.roll(even, PACK, 2)
    turned_odd = pltpu.roll(odd, PACK, 2)
    left = jnp.where(low, even, turned_odd)
    right = jnp.where(low, turned_even, odd)
    return jnp.concatenate([left[:, 0:8], right[:, 0:8], left[:, 8:16], right[:, 8:16]], axis=1)


def turn_kernel(merge, send, *refs):
    refs = list(refs)
    h_ref = refs.pop(0)
    if merge:
        back_ref, row_ref = refs.pop(0), refs.pop(0)
    if send:
        col_ref = refs.pop(0)
    hnew_ref = refs.pop(0)
    features, tokens = h_ref.shape
    held = h_ref[...]
    if merge:
        tiles = unpack_pairs(back_ref[...].astype(jnp.float32)).astype(jnp.bfloat16)
        offset = lax.broadcasted_iota(jnp.int32, (4 * PACK, tokens), 0)
        first, second = row_ref[0:1, :] - offset, row_ref[1:2, :] - offset
        update = jnp.zeros((32, tokens), jnp.float32)
        for turn in range(tiles.shape[0] // 2):
            base = turn * 4 * PACK
            onehot = jnp.where((first == base) | (second == base), 1.0, 0.0)
            pair = jnp.concatenate([tiles[2 * turn], tiles[2 * turn + 1]], axis=1)
            update += jnp.dot(
                pair, onehot.astype(jnp.bfloat16), preferred_element_type=jnp.float32
            )
        change = update[0:features] * (1.0 / update[features:features + 1])
        held = (held.astype(jnp.float32) + change).astype(jnp.bfloat16)
    hnew_ref[...] = held
    if send:
        out_ref = refs.pop(0)
        offset = lax.broadcasted_iota(jnp.int32, (tokens, 4 * PACK), 1)
        first, second = col_ref[:, 0:1] - offset, col_ref[:, 1:2] - offset
        low = lax.broadcasted_iota(jnp.int32, (8, 2 * PACK), 1) < PACK
        for turn in range(out_ref.shape[0] // 4):
            base = turn * 4 * PACK
            onehot = jnp.where((first == base) | (second == base), 1.0, 0.0)
            found = jnp.dot(held, onehot.astype(jnp.bfloat16), preferred_element_type=jnp.float32)
            for half in range(2):
                tile = found[:, 2 * PACK * half : 2 * PACK * (half + 1)]
                top, middle, bottom = tile[0:8], tile[8:16], tile[16:24]
                even = [jnp.where(low, top, pltpu.roll(middle, PACK, 1)), bottom]
                odd = [jnp.where(low, pltpu.roll(top, PACK, 1), middle), pltpu.roll(bottom, PACK, 1)]
                number = turn * 4 + half * 2
                out_ref[number] = jnp.concatenate(even, axis=0).astype(jnp.bfloat16)
                out_ref[number + 1] = jnp.concatenate(odd, axis=0).astype(jnp.bfloat16)


def run_turn(experts, h, back, rows, cols, before, after):
    features, tokens = h.shape
    merge, send = before is not None, after is not None
    operands, specs = [h], [VMEM]
    shapes, outs = [jax.ShapeDtypeStruct(h.shape, h.dtype)], [VMEM]
    if merge:
        operands += [back, rows]
        specs += [VMEM, plane((8, tokens), before)]
    if send:
        operands += [cols]
        specs += [plane((tokens, 2), after)]
        shapes += [jax.ShapeDtypeStruct((experts, 16, 2 * PACK), jnp.bfloat16)]
        outs += [VMEM]
    return pl.pallas_call(
        functools.partial(turn_kernel, merge, send),
        out_shape=tuple(shapes),
        grid=(1,),
        in_specs=specs,
        out_specs=tuple(outs),
        compiler_params=pltpu.CompilerParams(vmem_limit_bytes=VMEM_LIMIT),
        name="turn",
    )(*operands)


def expert_kernel(
    scal_ref, blocks_ref, gain_ref, router_ref, lane_ref, other_ref, out_ref,
    win_ref, wout_ref, sems,
):
    core = scal_ref[0]

    @pl.when(core == 0)
    def _():
        pltpu.make_async_copy(lane_ref, win_ref, sems.at[0]).start()
        pltpu.make_async_copy(other_ref, wout_ref, sems.at[1]).start()

    @pl.when(core != 0)
    def _():
        pltpu.make_async_copy(other_ref, win_ref, sems.at[0]).start()
        pltpu.make_async_copy(lane_ref, wout_ref, sems.at[1]).start()

    width = win_ref.shape[1]
    groups = blocks_ref.shape[0]
    blocks = blocks_ref[...].astype(jnp.float32)
    top, bottom = blocks[:, 0:8], blocks[:, 8:16]
    parts = [top[:, None], pltpu.roll(top, PACK, 2)[:, None], bottom[:, None]]
    tall = jnp.concatenate(parts, axis=1).reshape(width, 2 * PACK)
    wide = tall.T[0:PACK]
    mean_square = jnp.mean(wide * wide, axis=1, keepdims=True)
    normed = (wide * lax.rsqrt(mean_square + 1e-06) * gain_ref[...]).astype(jnp.bfloat16)
    logit = jnp.sum(normed.astype(jnp.float32) * router_ref[...], axis=1, keepdims=True)
    gate = jax.nn.sigmoid(logit).astype(jnp.bfloat16).astype(jnp.float32)
    pltpu.make_async_copy(lane_ref, win_ref, sems.at[0]).wait()
    pre_act = lax.dot_general(
        normed, win_ref[...], (((1,), (1,)), ((), ())), preferred_element_type=jnp.float32
    )
    active = jax.nn.gelu(pre_act, approximate=True).astype(jnp.bfloat16)
    pltpu.make_async_copy(lane_ref, wout_ref, sems.at[1]).wait()
    output = jnp.dot(active, wout_ref[...], preferred_element_type=jnp.float32)
    weighted = output * gate
    spread = jnp.broadcast_to(gate, (PACK, 2 * PACK))
    zeros = jnp.zeros_like(weighted)
    tall = jnp.concatenate([weighted, zeros], axis=0).T.reshape(groups, 3, 8, 2 * PACK)
    gates = jnp.concatenate([spread, jnp.zeros_like(spread)], axis=0).T[0:8]
    gates = jnp.broadcast_to(pltpu.roll(gates, PACK, 1)[None], (groups, 8, 2 * PACK))
    low = lax.broadcasted_iota(jnp.int32, (1, 1, 2 * PACK), 2) < PACK
    first = jnp.where(low, tall[:, 0], pltpu.roll(tall[:, 1], PACK, 2))
    second = jnp.where(low, tall[:, 2], gates)
    out_ref[...] = jnp.concatenate([first, second], axis=1).astype(jnp.bfloat16)


def run_expert(layer, scal, blocks, gains, routers, lane_w, other_w):
    hidden, width = lane_w.shape
    return pl.pallas_call(
        expert_kernel,
        out_shape=jax.ShapeDtypeStruct(blocks.shape, jnp.bfloat16),
        grid=(1,),
        in_specs=[SMEM, VMEM, plane((1, width), layer), plane((1, width), layer), HBM, HBM],
        out_specs=VMEM,
        scratch_shapes=[
            pltpu.VMEM((hidden, width), jnp.bfloat16),
            pltpu.VMEM((hidden, width), jnp.bfloat16),
            pltpu.SemaphoreType.DMA((2,)),
        ],
        compiler_params=pltpu.CompilerParams(vmem_limit_bytes=VMEM_LIMIT),
        cost_estimate=pl.CostEstimate(
            flops=4 * PACK * hidden * width, bytes_accessed=4 * hidden * width, transcendentals=0
        ),
        name="expert",
    )(scal, blocks, gains, routers, lane_w, other_w)


def plane(shape, *lead):
    return pl.BlockSpec((None,) * len(lead) + shape, lambda i: lead + (0,) * len(shape))


def place_tokens(routes, experts):
    tokens = routes.shape[1]
    ids = jnp.arange(experts, dtype=jnp.int32)
    first = routes[:, :, 0:1] == ids
    second = routes[:, :, 1:2] == ids
    named = (first | second).astype(jnp.bfloat16)
    earlier = jnp.tril(jnp.ones((tokens, tokens), jnp.bfloat16), -1)
    rank = jnp.einsum("ut,lte->lue", earlier, named, preferred_element_type=jnp.float32)
    rank = rank.astype(jnp.int32) + ids * PACK
    slot_first = jnp.sum(jnp.where(first, rank, 0), axis=2)
    slot_second = jnp.sum(jnp.where(second, rank, 0), axis=2)
    cols = jnp.stack([slot_first, slot_second], axis=2)
    blank = jnp.zeros_like(slot_first)
    rows = jnp.stack([slot_first, slot_second] + [blank] * 6, axis=1)
    return cols, rows


def join(*values):
    return lax.optimization_barrier(values)


def local(inputs, routes, norm_gains, routers, expert_in, expert_out):
    sections = lax.axis_size("section")
    experts = lax.axis_size("expert")
    section_pos = lax.axis_index("section")
    repeats, _, _, hidden, width = expert_in.shape
    layers = repeats * sections
    phases, held = ring_plan(sections, layers, PARTS, LEAD, SKIP)
    size = hidden // PARTS
    scal = jnp.stack([section_pos % 2, section_pos]).astype(jnp.int32)

    buffers = {("in", r): (expert_in, (r, 0, 0)) for r in range(repeats)}
    buffers.update({("out", r): (expert_out, (r, 0, 0)) for r in range(repeats)})
    every = [(lane, y) for lane in range(2) for y in range(sections // 2)]
    table, wanted = [], []

    def source_of(lane, y, i):
        q, part = i // PARTS, i % PARTS
        if q % sections // 2 != y:
            return ("ring", held[lane][y][i]), 0
        name = ("in", "out")[lane] if q % 2 == lane else "swapped"
        return (name, q // sections), part * size

    def add_pick(by_section):
        choices = sorted(set(by_section.values()))
        table.append([choices.index(by_section.get(s, choices[0])) for s in range(sections)])
        wanted.append(choices)
        return len(table) - 1

    swap_rows = [
        [
            add_pick({2 * y + lane: ((("out", "in")[lane], r), part * size) for lane, y in every})
            for part in range(PARTS)
        ]
        for r in range(repeats)
    ]
    ring_rows = [
        [add_pick({2 * y + lane: source_of(lane, y, i) for lane, y, _, i in moves})] if moves else []
        for moves in phases
    ]
    layer_rows = [
        [
            add_pick({2 * y + lane: source_of(lane, y, q * PARTS + part) for lane, y in every})
            for part in range(PARTS)
        ]
        for q in range(layers)
    ]
    tab = jnp.asarray(np.array(table, np.int32).T)[section_pos]

    def picked(rows, tab):
        names = sorted({name for row in rows for name, _ in wanted[row]})
        found = [buffers[name] for name in names]
        plan = tuple(
            (row, tuple((names.index(name), start) for name, start in wanted[row])) for row in rows
        )
        return pick(tab, plan, [array for array, _ in found], [place for _, place in found], size, width)

    def swapped(value):
        return lax.ppermute(value, "section", [(s, s ^ 1) for s in range(sections)])

    def ring(phase, tab):
        if phase > len(phases) or not phases[phase - 1]:
            return None
        pairs = [(2 * y + lane, 2 * target + lane) for lane, y, target, _ in phases[phase - 1]]
        return lax.ppermute(picked(ring_rows[phase - 1], tab), "section", pairs)

    def arrival(q):
        parts = range(q * PARTS, (q + 1) * PARTS)
        return max(stock[i] for lane in held for stock in lane for i in parts)

    mine = lax.all_to_all(routes[:, 0], "section", split_axis=1, concat_axis=0, tiled=False)
    mine = jnp.transpose(mine, (1, 0, 2, 3)).reshape(layers, -1, 2)
    cols, rows = place_tokens(mine, experts)
    small = jnp.stack([norm_gains[:, 0], routers[:, 0, 0]])
    small = jnp.broadcast_to(small[None], (sections,) + small.shape)
    small = lax.all_to_all(small, "section", split_axis=0, concat_axis=0, tiled=True)
    small = jnp.transpose(small, (1, 2, 0, 3)).reshape(2, layers, 1, width).astype(jnp.float32)
    gains, gate_rows = small[0], small[1]
    h = jnp.transpose(inputs[0], (1, 0))

    buffers[("swapped", 0)] = (swapped(picked(swap_rows[0], tab)), ())
    later = swapped(picked(swap_rows[1], tab))
    flying = None
    for phase in range(1, LEAD):
        arrived = ring(phase, tab)
        if phase == 1:
            arrived, later, tab = join(arrived, later, tab)
            buffers[("swapped", 1)] = (later, ())
        else:
            arrived, tab = join(arrived, tab)
        buffers[("ring", phase)] = (arrived, ())
    tab, cols, rows, gains, gate_rows, h = join(tab, cols, rows, gains, gate_rows, h)

    def run_phase(phase, value, tab, flying, wish):
        value, tab = join(value, tab)
        sent = lax.all_to_all(value, "expert", split_axis=0, concat_axis=0, tiled=True)
        lane_w = other_w = None
        if wish is not None:
            lane_w = picked(layer_rows[wish], tab)
            other_w = swapped(lane_w)
        started = ring(phase, tab)
        bundle = [v for v in (sent, lane_w, other_w, tab, flying) if v is not None]
        bundle = list(join(*bundle))
        sent = bundle.pop(0)
        if wish is not None:
            lane_w, other_w = bundle.pop(0), bundle.pop(0)
        tab = bundle.pop(0)
        if flying is not None:
            buffers[("ring", phase)] = (bundle.pop(0), ())
        return sent, tab, started, lane_w, other_w

    back = None
    for q in range(layers):
        first, second = LEAD + 2 * q, LEAD + 2 * q + 1
        h, blocks = run_turn(
            experts, h, back, rows, cols, q - 1 if q else None, q
        )
        wish = q if arrival(q) < first else None
        blocks, tab, flying, lane_w, other_w = run_phase(first, blocks, tab, flying, wish)
        if wish is None:
            lane_w = picked(layer_rows[q], tab)
            other_w = swapped(lane_w)
        back = run_expert(q, scal, blocks, gains, gate_rows, lane_w, other_w)
        back, tab, flying, _, _ = run_phase(second, back, tab, flying, None)

    (h,) = run_turn(experts, h, back, rows, cols, layers - 1, None)
    return jnp.transpose(h, (1, 0))[None]


def solution(mesh):
    return jax.shard_map(
        local,
        mesh=mesh,
        in_specs=(
            P("section", None, "expert"),
            P(None, "section", None, None, None),
            P(None, "section", None),
            P(None, "section", "expert", None),
            P(None, "section", "expert", None, None),
            P(None, "section", "expert", None, None),
        ),
        out_specs=P("section", None, "expert"),
        check_vma=False,
    )
```

```python
import functools

import jax
import jax.numpy as jnp
import numpy as np
from jax import lax
from jax.experimental import pallas as pl
from jax.experimental.pallas import tpu as pltpu
from jax.sharding import PartitionSpec as P

VMEM_LIMIT = 62 * 1024 * 1024
HBM = pl.BlockSpec(memory_space=pltpu.HBM)
SMEM = pl.BlockSpec(memory_space=pltpu.SMEM)
VMEM = pl.BlockSpec(memory_space=pltpu.VMEM)
DIRS = (1, -1)


PACK = 64
SLOTS = 48
ROWS = 10
PARTS = 2
LEAD = 8


def ring_plan(sections, layers, parts):
    chips = sections // 2
    items = layers * parts
    owned = [[i for i in range(items) if (i // parts) % sections // 2 == y] for y in range(chips)]
    held = [[dict.fromkeys(owned[y], 0) for y in range(chips)] for _ in DIRS]
    phases = []
    while any(len(stock) < items for lane in held for stock in lane):
        number = len(phases) + 1
        moves = []
        for lane, step in enumerate(DIRS):
            for y in range(chips):
                target = (y + step) % chips
                options = [i for i, at in held[lane][y].items() if at < number]
                options = [i for i in options if i not in held[lane][target]]
                if options:
                    moves.append((lane, y, target, min(options)))
        phases.append(moves)
        for lane, y, target, i in moves:
            held[lane][target][i] = number + 1
    return phases, held


class Side:
    def __init__(self, tab, jobs, size, width):
        self.jobs, self.size, self.width = jobs, size, width
        found = {name: place for job in jobs for name, place in job["sources"].items()}
        self.names = sorted(found)
        self.places = [found[name][1] for name in self.names]
        self.operands = [tab] + [found[name][0] for name in self.names] if jobs else []
        self.in_specs = [SMEM] + [HBM] * len(self.names) if jobs else []
        self.shapes, self.out_specs, self.scratch = [], [], []
        for job in jobs:
            shape = (size * len(job["rows"]), width)
            self.shapes.append(jax.ShapeDtypeStruct(shape, jnp.bfloat16))
            self.out_specs.append(HBM)
            self.scratch.append(pltpu.VMEM(shape, jnp.bfloat16))
            self.scratch.append(pltpu.SemaphoreType.DMA((len(job["rows"]),)))
            self.scratch.append(pltpu.SemaphoreType.DMA((len(job["rows"]),)))

    def bind(self, inputs, outputs, scratch):
        self.inputs, self.outputs, self.holds = inputs, outputs, scratch

    def view(self, name, start):
        number = self.names.index(name)
        place = self.places[number] + (pl.ds(start, self.size),)
        return self.inputs[1 + number].at[place]

    def parts(self):
        for number, job in enumerate(self.jobs):
            hold, in_sems, out_sems = self.holds[3 * number : 3 * number + 3]
            for part, (row, choices) in enumerate(job["rows"]):
                at = pl.ds(part * self.size, self.size)
                target = self.outputs[number].at[at]
                yield row, choices, hold.at[at], target, in_sems.at[part], out_sems.at[part]

    def begin(self):
        for row, choices, hold, _, in_sem, _ in self.parts():
            choice = self.inputs[0][row]
            for number, (name, start) in enumerate(choices):

                @pl.when(choice == number)
                def _(name=name, start=start, hold=hold, in_sem=in_sem):
                    pltpu.make_async_copy(self.view(name, start), hold, in_sem).start()

    def middle(self):
        for _, choices, hold, target, in_sem, out_sem in self.parts():
            pltpu.make_async_copy(self.view(*choices[0]), hold, in_sem).wait()
            pltpu.make_async_copy(hold, target, out_sem).start()

    def finish(self):
        for _, _, hold, target, _, out_sem in self.parts():
            pltpu.make_async_copy(hold, target, out_sem).wait()


def call_with_side(kernel, side, operands, in_specs, shapes, out_specs, scratch, **options):
    n_in, n_side = len(operands), len(side.operands)
    n_out, n_scratch = len(shapes), len(scratch)

    def body(*refs):
        refs = list(refs)

        def take(count):
            taken = refs[:count]
            del refs[:count]
            return taken

        ins, side_ins = take(n_in), take(n_side)
        outs, side_outs = take(n_out), take(len(side.shapes))
        own = take(n_scratch)
        side.bind(side_ins, side_outs, refs)
        kernel(side, *ins, *outs, *own)

    return pl.pallas_call(
        body,
        out_shape=tuple(shapes) + tuple(side.shapes),
        grid=(1,),
        in_specs=list(in_specs) + side.in_specs,
        out_specs=tuple(out_specs) + tuple(side.out_specs),
        scratch_shapes=list(scratch) + side.scratch,
        compiler_params=pltpu.CompilerParams(vmem_limit_bytes=VMEM_LIMIT),
        **options,
    )(*operands, *side.operands)


def copy_kernel(side):
    side.begin()
    side.middle()
    side.finish()


LANES = 128


def turned(value, lanes):
    return pltpu.roll(value, lanes % LANES, value.ndim - 1)


def lanes_of(value):
    return lax.broadcasted_iota(jnp.int32, (1,) * (value.ndim - 1) + (LANES,), value.ndim - 1)


def fold_tail(third, at):
    axis = third.ndim - 1
    spread = pltpu.roll(turned(third, -at - 32), 0, axis, stride=16, stride_axis=axis - 1)
    place = lax.broadcasted_iota(jnp.int32, third.shape, axis) // 16
    own = place == lax.broadcasted_iota(jnp.int32, third.shape, axis - 1)
    return jnp.sum(jnp.where(own, spread, 0.0), axis=axis - 1, keepdims=True)


def unfold_tail(row, at):
    value = jnp.broadcast_to(turned(row, at + 32), row.shape[:-2] + (8, LANES))
    number = lax.broadcasted_iota(jnp.int32, value.shape, value.ndim - 2)
    for step in (1, 2, 4):
        value = jnp.where((number & step) != 0, turned(value, -16 * step), value)
    return value


def pack(first, second, third, at, gates=None):
    lanes = lanes_of(first)
    top = jnp.where(
        lanes < SLOTS,
        turned(first, -at),
        jnp.where(lanes < 2 * SLOTS, turned(second, SLOTS - at), turned(third, 2 * SLOTS - at)),
    )
    tail = fold_tail(third, at)
    axis = first.ndim - 2
    number = lax.broadcasted_iota(jnp.int32, top.shape, axis)
    last = jnp.broadcast_to(tail, top.shape)
    if gates is not None:
        last = jnp.where(number == 0, last, gates)
    return jnp.concatenate([top, last], axis=axis)


def unpack(blocks, at):
    top, last = blocks[..., 0:8, :], blocks[..., 8:16, :]
    lanes = lanes_of(blocks)
    third = jnp.where(
        lanes - at < 32, turned(top, at - 2 * SLOTS), unfold_tail(last[..., 0:1, :], at)
    )
    return turned(top, at), turned(top, at - SLOTS), third, turned(last, at)


def unpack_pairs(back):
    pairs = back.shape[0] // 2
    split = back.reshape(pairs, 2, 16, LANES)
    low = lanes_of(back) < PACK
    both = zip(unpack(split[:, 0], 0), unpack(split[:, 1], PACK))
    groups = [jnp.where(low, even, odd) for even, odd in both]
    gates = jnp.broadcast_to(groups[3][:, 1:2], groups[0].shape)
    return jnp.concatenate(groups[0:3] + [gates], axis=1)


def send_blocks(value):
    count = value.shape[0]
    packed = value[:, 0:ROWS].reshape(count * ROWS // 2, 2, LANES)
    sent = lax.all_to_all(packed, "expert", split_axis=0, concat_axis=0, tiled=True)
    return jnp.pad(sent.reshape(count, ROWS, LANES), ((0, 0), (0, 16 - ROWS), (0, 0)))


def turn_kernel(merge, send, side, *refs):
    side.begin()
    refs = list(refs)
    h_ref = refs.pop(0)
    if merge:
        back_ref, row_ref = refs.pop(0), refs.pop(0)
    if send:
        next_ref = refs.pop(0)
    hnew_ref = refs.pop(0)
    features, tokens = h_ref.shape
    held = h_ref[...]
    if merge:
        tiles = unpack_pairs(back_ref[...].astype(jnp.float32)).astype(jnp.bfloat16)
        offset = lax.broadcasted_iota(jnp.int32, (4 * PACK, tokens), 0)
        first, second = row_ref[0:1, :] - offset, row_ref[1:2, :] - offset
        update = jnp.zeros((32, tokens), jnp.float32)
        for turn in range(tiles.shape[0] // 2):
            base = turn * 4 * PACK
            onehot = jnp.where((first == base) | (second == base), 1.0, 0.0)
            pair = jnp.concatenate([tiles[2 * turn], tiles[2 * turn + 1]], axis=1)
            update += jnp.dot(
                pair, onehot.astype(jnp.bfloat16), preferred_element_type=jnp.float32
            )
        change = update[0:features] * (1.0 / update[features:features + 1])
        held = (held.astype(jnp.float32) + change).astype(jnp.bfloat16)
    hnew_ref[...] = held
    side.middle()
    if send:
        out_ref = refs.pop(0)
        offset = lax.broadcasted_iota(jnp.int32, (tokens, 4 * PACK), 1)
        col = next_ref[...].astype(jnp.float32).T.astype(jnp.int32)
        first, second = col[:, 0:1] - offset, col[:, 1:2] - offset
        for turn in range(out_ref.shape[0] // 4):
            base = turn * 4 * PACK
            onehot = jnp.where((first == base) | (second == base), 1.0, 0.0)
            found = jnp.dot(held, onehot.astype(jnp.bfloat16), preferred_element_type=jnp.float32)
            for half in range(2):
                tile = found[:, LANES * half : LANES * (half + 1)]
                groups = tile[0:8], tile[8:16], tile[16:24]
                number = turn * 4 + half * 2
                out_ref[number] = pack(*groups, 0).astype(jnp.bfloat16)
                out_ref[number + 1] = pack(*groups, PACK).astype(jnp.bfloat16)
    side.finish()


def run_turn(side, experts, h, back, rows, before, after):
    features, tokens = h.shape
    merge, send = before is not None, after is not None
    operands, specs = [h], [VMEM]
    shapes, outs = [jax.ShapeDtypeStruct(h.shape, h.dtype)], [VMEM]
    if merge:
        operands += [back, rows]
        specs += [VMEM, plane((8, tokens), before)]
    if send:
        operands += [rows]
        specs += [plane((8, tokens), after)]
        shapes += [jax.ShapeDtypeStruct((experts, 16, LANES), jnp.bfloat16)]
        outs += [VMEM]
    return call_with_side(
        functools.partial(turn_kernel, merge, send), side, operands, specs, shapes, outs, [],
        name="turn",
    )


def expert_kernel(
    side, scal_ref, blocks_ref, gain_ref, router_ref, lane_ref, other_ref, out_ref,
    win_ref, wout_ref, sems,
):
    core = scal_ref[0]

    @pl.when(core == 0)
    def _():
        pltpu.make_async_copy(lane_ref, win_ref, sems.at[0]).start()
        pltpu.make_async_copy(other_ref, wout_ref, sems.at[1]).start()

    @pl.when(core != 0)
    def _():
        pltpu.make_async_copy(other_ref, win_ref, sems.at[0]).start()
        pltpu.make_async_copy(lane_ref, wout_ref, sems.at[1]).start()

    side.begin()
    width = win_ref.shape[1]
    groups = blocks_ref.shape[0]
    blocks = blocks_ref[...].astype(jnp.float32)
    parts = [group[:, None] for group in unpack(blocks, 0)[0:3]]
    tall = jnp.concatenate(parts, axis=1).reshape(width, LANES)
    wide = tall.T[0:PACK]
    mean_square = jnp.mean(wide * wide, axis=1, keepdims=True)
    normed = (wide * lax.rsqrt(mean_square + 1e-06) * gain_ref[...]).astype(jnp.bfloat16)
    logit = jnp.sum(normed.astype(jnp.float32) * router_ref[...], axis=1, keepdims=True)
    gate = jax.nn.sigmoid(logit).astype(jnp.bfloat16).astype(jnp.float32)
    pltpu.make_async_copy(lane_ref, win_ref, sems.at[0]).wait()
    pre_act = lax.dot_general(
        normed, win_ref[...], (((1,), (1,)), ((), ())), preferred_element_type=jnp.float32
    )
    side.middle()
    active = jax.nn.gelu(pre_act, approximate=True).astype(jnp.bfloat16)
    pltpu.make_async_copy(lane_ref, wout_ref, sems.at[1]).wait()
    output = jnp.dot(active, wout_ref[...], preferred_element_type=jnp.float32)
    weighted = output * gate
    spread = jnp.broadcast_to(gate, (PACK, LANES))
    zeros = jnp.zeros_like(weighted)
    tall = jnp.concatenate([weighted, zeros], axis=0).T.reshape(groups, 3, 8, LANES)
    gates = jnp.concatenate([spread, jnp.zeros_like(spread)], axis=0).T[0:8]
    gates = jnp.broadcast_to(gates[None], (groups, 8, LANES))
    out_ref[...] = pack(tall[:, 0], tall[:, 1], tall[:, 2], 0, gates).astype(jnp.bfloat16)
    side.finish()


def run_expert(side, layer, scal, blocks, gains, routers, lane_w, other_w):
    hidden, width = lane_w.shape
    return call_with_side(
        expert_kernel,
        side,
        [scal, blocks, gains, routers, lane_w, other_w],
        [SMEM, VMEM, plane((1, width), layer), plane((1, width), layer), HBM, HBM],
        [jax.ShapeDtypeStruct(blocks.shape, jnp.bfloat16)],
        [VMEM],
        [
            pltpu.VMEM((hidden, width), jnp.bfloat16),
            pltpu.VMEM((hidden, width), jnp.bfloat16),
            pltpu.SemaphoreType.DMA((2,)),
        ],
        cost_estimate=pl.CostEstimate(
            flops=4 * PACK * hidden * width, bytes_accessed=4 * hidden * width, transcendentals=0
        ),
        name="expert",
    )


def plane(shape, *lead):
    return pl.BlockSpec((None,) * len(lead) + shape, lambda i: lead + (0,) * len(shape))


def place_tokens(routes, experts):
    tokens = routes.shape[1]
    ids = jnp.arange(experts, dtype=jnp.int32)
    first = routes[:, :, 0:1] == ids
    second = routes[:, :, 1:2] == ids
    named = (first | second).astype(jnp.bfloat16)
    earlier = jnp.tril(jnp.ones((tokens, tokens), jnp.bfloat16), -1)
    rank = jnp.einsum("ut,lte->lue", earlier, named, preferred_element_type=jnp.float32)
    rank = rank.astype(jnp.int32) + ids * PACK
    slot_first = jnp.sum(jnp.where(first, rank, 0), axis=2)
    slot_second = jnp.sum(jnp.where(second, rank, 0), axis=2)
    blank = jnp.zeros_like(slot_first)
    return jnp.stack([slot_first, slot_second] + [blank] * 6, axis=1)


def join(*values):
    return lax.optimization_barrier(values)


def local(inputs, routes, norm_gains, routers, expert_in, expert_out):
    sections = lax.axis_size("section")
    experts = lax.axis_size("expert")
    section_pos = lax.axis_index("section")
    repeats, _, _, hidden, width = expert_in.shape
    layers = repeats * sections
    phases, held = ring_plan(sections, layers, PARTS)
    size = hidden // PARTS
    scal = jnp.stack([section_pos % 2, section_pos]).astype(jnp.int32)

    buffers = {("in", r): (expert_in, (r, 0, 0)) for r in range(repeats)}
    buffers.update({("out", r): (expert_out, (r, 0, 0)) for r in range(repeats)})
    every = [(lane, y) for lane in range(2) for y in range(sections // 2)]
    table, wanted = [], []

    def source_of(lane, y, i):
        q, part = i // PARTS, i % PARTS
        if q % sections // 2 != y:
            return ("ring", held[lane][y][i]), 0
        name = ("in", "out")[lane] if q % 2 == lane else "swapped"
        return (name, q // sections), part * size

    def add_pick(by_section):
        choices = sorted(set(by_section.values()))
        table.append([choices.index(by_section.get(s, choices[0])) for s in range(sections)])
        wanted.append(choices)
        return len(table) - 1

    swap_rows = [
        [
            add_pick({2 * y + lane: ((("out", "in")[lane], r), part * size) for lane, y in every})
            for part in range(PARTS)
        ]
        for r in range(repeats)
    ]
    ring_rows = [
        [add_pick({2 * y + lane: source_of(lane, y, i) for lane, y, _, i in moves})] if moves else []
        for moves in phases
    ]
    layer_rows = [
        [
            add_pick({2 * y + lane: source_of(lane, y, q * PARTS + part) for lane, y in every})
            for part in range(PARTS)
        ]
        for q in range(layers)
    ]
    tab = jnp.asarray(np.array(table, np.int32).T)[section_pos]

    def job(rows):
        names = sorted({name for row in rows for name, _ in wanted[row]})
        return {
            "sources": {name: buffers[name] for name in names},
            "rows": [(row, wanted[row]) for row in rows],
        }

    def side(*rows):
        return Side(tab, [job(some) for some in rows if some], size, width)

    def picked(rows):
        (value,) = call_with_side(copy_kernel, side(rows), [], [], [], [], [], name="pick")
        return value

    def swapped(value):
        return lax.ppermute(value, "section", [(s, s ^ 1) for s in range(sections)])

    def ring_row(phase):
        return ring_rows[phase - 1] if phase <= len(phases) else []

    def ring(phase, value):
        pairs = [(2 * y + lane, 2 * target + lane) for lane, y, target, _ in phases[phase - 1]]
        return lax.ppermute(value, "section", pairs)

    def arrival(q):
        parts = range(q * PARTS, (q + 1) * PARTS)
        return max(stock[i] for lane in held for stock in lane for i in parts)

    mine = lax.all_to_all(routes[:, 0], "section", split_axis=1, concat_axis=0, tiled=False)
    mine = jnp.transpose(mine, (1, 0, 2, 3)).reshape(layers, -1, 2)
    rows = place_tokens(mine, experts)
    small = jnp.stack([norm_gains[:, 0], routers[:, 0, 0]])
    small = jnp.broadcast_to(small[None], (sections,) + small.shape)
    small = lax.all_to_all(small, "section", split_axis=0, concat_axis=0, tiled=True)
    small = jnp.transpose(small, (1, 2, 0, 3)).reshape(2, layers, 1, width).astype(jnp.float32)
    gains, gate_rows = small[0], small[1]
    h = jnp.transpose(inputs[0], (1, 0))

    buffers[("swapped", 0)] = (swapped(picked(swap_rows[0])), ())
    later = swapped(picked(swap_rows[1]))
    flying = None
    for phase in range(1, LEAD):
        started = ring(phase, picked(ring_row(phase)))
        if flying is not None:
            flying, tab = join(flying, tab)
            buffers[("ring", phase)] = (flying, ())
        if phase == 2:
            later, tab = join(later, tab)
            buffers[("swapped", 1)] = (later, ())
        flying = started
    tab, rows, gains, gate_rows, h = join(tab, rows, gains, gate_rows, h)

    def wish_of(phase):
        for q in range(layers):
            first = LEAD + 2 * q
            if phase == first - 1 and arrival(q) < first - 1:
                return q
            if phase == first and first - 1 <= arrival(q) < first:
                return q
        return None

    def sides(phase):
        wish = wish_of(phase)
        return wish, side([] if wish is None else layer_rows[wish], ring_row(phase))

    ready = {}

    def run_phase(phase, wish, value, flying, extra):
        extra = list(extra)
        bundle = [send_blocks(value)]
        if wish is not None:
            lane_w = extra.pop(0)
            bundle += [lane_w, swapped(lane_w)]
        started = ring(phase, extra.pop(0)) if extra else None
        if flying is not None:
            bundle.append(flying)
        bundle = list(join(*bundle))
        if flying is not None:
            buffers[("ring", phase)] = (bundle.pop(), ())
        if wish is not None:
            ready[wish] = (bundle[1], bundle[2])
        return bundle[0], started

    back = None
    for q in range(layers):
        first = LEAD + 2 * q
        wish, beside = sides(first)
        before = q - 1 if q else None
        h, blocks, *extra = run_turn(beside, experts, h, back, rows, before, q)
        blocks, flying = run_phase(first, wish, blocks, flying, extra)
        if q not in ready:
            lane_w = picked(layer_rows[q])
            ready[q] = (lane_w, swapped(lane_w))
        wish, beside = sides(first + 1)
        back, *extra = run_expert(beside, q, scal, blocks, gains, gate_rows, *ready.pop(q))
        back, flying = run_phase(first + 1, wish, back, flying, extra)

    (h,) = run_turn(side(), experts, h, back, rows, layers - 1, None)
    return jnp.transpose(h, (1, 0))[None]


def solution(mesh):
    return jax.shard_map(
        local,
        mesh=mesh,
        in_specs=(
            P("section", None, "expert"),
            P(None, "section", None, None, None),
            P(None, "section", None),
            P(None, "section", "expert", None),
            P(None, "section", "expert", None, None),
            P(None, "section", "expert", None, None),
        ),
        out_specs=P("section", None, "expert"),
        check_vma=False,
    )
```

```python
import functools

import jax
import jax.numpy as jnp
import numpy as np
from jax import lax
from jax.experimental import pallas as pl
from jax.experimental.pallas import tpu as pltpu
from jax.sharding import PartitionSpec as P

VMEM_LIMIT = 62 * 1024 * 1024
HBM = pl.BlockSpec(memory_space=pltpu.HBM)
SMEM = pl.BlockSpec(memory_space=pltpu.SMEM)
VMEM = pl.BlockSpec(memory_space=pltpu.VMEM)
DIRS = (1, -1)


PACK = 64
SLOTS = 48
ROWS = 10
PARTS = 2
LEAD = 6


def ring_plan(sections, layers, parts, lead):
    chips = sections // 2
    items = layers * parts
    held = [
        [
            {i: (0, 0, 0) for i in range(items) if (i // parts) % sections // 2 == y}
            for y in range(chips)
        ]
        for _ in DIRS
    ]
    steps = []
    while any(len(stock) < items for lane in held for stock in lane):
        number = len(steps) + 1
        moves = []
        for lane, step in enumerate(DIRS):
            for y in range(chips):
                target = (y + step) % chips
                there = held[lane][target]
                options = sorted(i for i, at in held[lane][y].items() if at[0] < number and i not in there)
                for place, i in enumerate(options[: 1 if number <= lead else parts]):
                    moves.append((lane, y, target, i, place))
        steps.append(moves)
        for lane, _, target, i, place in moves:
            held[lane][target][i] = (number + (number < lead), number, place)
    return steps, held


def pick_kernel(rows, places, tab_ref, *refs):
    count = len(places)
    sources, (out_ref, hold_ref, in_sems, out_sems) = refs[:count], refs[count:]
    size = hold_ref.shape[0] // len(rows)

    def view(number, start):
        return sources[number].at[places[number] + (pl.ds(start, size),)]

    def part_of(ref, part):
        return ref.at[pl.ds(part * size, size)]

    for part, (row, choices) in enumerate(rows):
        choice = tab_ref[row]
        for number, (source, start) in enumerate(choices):

            @pl.when(choice == number)
            def _(part=part, source=source, start=start):
                pltpu.make_async_copy(
                    view(source, start), part_of(hold_ref, part), in_sems.at[part]
                ).start()

    def leave(part):
        return pltpu.make_async_copy(
            part_of(hold_ref, part), part_of(out_ref, part), out_sems.at[part]
        )

    for part, (_, choices) in enumerate(rows):
        pltpu.make_async_copy(
            view(*choices[0]), part_of(hold_ref, part), in_sems.at[part]
        ).wait()
        leave(part).start()
    for part in range(len(rows)):
        leave(part).wait()


def pick(tab, rows, sources, places, size, width):
    shape = (size * len(rows), width)
    return pl.pallas_call(
        functools.partial(pick_kernel, rows, places),
        out_shape=jax.ShapeDtypeStruct(shape, jnp.bfloat16),
        in_specs=[SMEM] + [HBM] * len(sources),
        out_specs=HBM,
        scratch_shapes=[
            pltpu.VMEM(shape, jnp.bfloat16),
            pltpu.SemaphoreType.DMA((len(rows),)),
            pltpu.SemaphoreType.DMA((len(rows),)),
        ],
        compiler_params=pltpu.CompilerParams(vmem_limit_bytes=VMEM_LIMIT),
        cost_estimate=pl.CostEstimate(
            flops=0, bytes_accessed=4 * shape[0] * width, transcendentals=0
        ),
        name="pick",
    )(tab, *sources)


LANES = 128


def turned(value, lanes):
    return pltpu.roll(value, lanes % LANES, value.ndim - 1)


def lanes_of(value):
    return lax.broadcasted_iota(jnp.int32, (1,) * (value.ndim - 1) + (LANES,), value.ndim - 1)


def fold_tail(third, at):
    axis = third.ndim - 1
    spread = pltpu.roll(turned(third, -at - 32), 0, axis, stride=16, stride_axis=axis - 1)
    place = lax.broadcasted_iota(jnp.int32, third.shape, axis) // 16
    own = place == lax.broadcasted_iota(jnp.int32, third.shape, axis - 1)
    return jnp.sum(jnp.where(own, spread, 0.0), axis=axis - 1, keepdims=True)


def unfold_tail(row, at):
    value = jnp.broadcast_to(turned(row, at + 32), row.shape[:-2] + (8, LANES))
    number = lax.broadcasted_iota(jnp.int32, value.shape, value.ndim - 2)
    for step in (1, 2, 4):
        value = jnp.where((number & step) != 0, turned(value, -16 * step), value)
    return value


def pack(first, second, third, at, gates=None):
    lanes = lanes_of(first)
    top = jnp.where(
        lanes < SLOTS,
        turned(first, -at),
        jnp.where(lanes < 2 * SLOTS, turned(second, SLOTS - at), turned(third, 2 * SLOTS - at)),
    )
    tail = fold_tail(third, at)
    axis = first.ndim - 2
    number = lax.broadcasted_iota(jnp.int32, top.shape, axis)
    last = jnp.broadcast_to(tail, top.shape)
    if gates is not None:
        last = jnp.where(number == 0, last, gates)
    return jnp.concatenate([top, last], axis=axis)


def unpack(blocks, at):
    top, last = blocks[..., 0:8, :], blocks[..., 8:16, :]
    lanes = lanes_of(blocks)
    third = jnp.where(
        lanes - at < 32, turned(top, at - 2 * SLOTS), unfold_tail(last[..., 0:1, :], at)
    )
    return turned(top, at), turned(top, at - SLOTS), third, turned(last, at)


def unpack_pairs(back):
    pairs = back.shape[0] // 2
    split = back.reshape(pairs, 2, 16, LANES)
    low = lanes_of(back) < PACK
    both = zip(unpack(split[:, 0], 0), unpack(split[:, 1], PACK))
    groups = [jnp.where(low, even, odd) for even, odd in both]
    gates = jnp.broadcast_to(groups[3][:, 1:2], groups[0].shape)
    return jnp.concatenate(groups[0:3] + [gates], axis=1)


TILES = ROWS // 2


def load_blocks(ref, wide_ref):
    for number in range(wide_ref.shape[0]):
        block = ref[TILES * number : TILES * (number + 1)].reshape(ROWS, LANES)
        wide_ref[number, 0:ROWS] = block.astype(jnp.float32)
    return wide_ref[...]


def store_block(ref, number, block):
    rows = block.astype(jnp.bfloat16).reshape(8, 2, LANES)
    ref[TILES * number : TILES * (number + 1)] = rows[0:TILES]


def send_blocks(value):
    return lax.all_to_all(value, "expert", split_axis=0, concat_axis=0, tiled=True)


def turn_kernel(merge, send, *refs):
    refs = list(refs)
    h_ref = refs.pop(0)
    if merge:
        back_ref, row_ref = refs.pop(0), refs.pop(0)
    if send:
        next_ref = refs.pop(0)
    hnew_ref = refs.pop(0)
    features, tokens = h_ref.shape
    held = h_ref[...]
    if merge:
        tiles = unpack_pairs(load_blocks(back_ref, refs.pop())).astype(jnp.bfloat16)
        offset = lax.broadcasted_iota(jnp.int32, (4 * PACK, tokens), 0)
        first, second = row_ref[0:1, :] - offset, row_ref[1:2, :] - offset
        update = jnp.zeros((32, tokens), jnp.float32)
        for turn in range(tiles.shape[0] // 2):
            base = turn * 4 * PACK
            onehot = jnp.where((first == base) | (second == base), 1.0, 0.0)
            pair = jnp.concatenate([tiles[2 * turn], tiles[2 * turn + 1]], axis=1)
            update += jnp.dot(
                pair, onehot.astype(jnp.bfloat16), preferred_element_type=jnp.float32
            )
        change = update[0:features] * (1.0 / update[features:features + 1])
        held = (held.astype(jnp.float32) + change).astype(jnp.bfloat16)
    hnew_ref[...] = held
    if send:
        out_ref = refs.pop(0)
        offset = lax.broadcasted_iota(jnp.int32, (tokens, 4 * PACK), 1)
        col = next_ref[...].astype(jnp.float32).T.astype(jnp.int32)
        first, second = col[:, 0:1] - offset, col[:, 1:2] - offset
        for turn in range(out_ref.shape[0] // TILES // 4):
            base = turn * 4 * PACK
            onehot = jnp.where((first == base) | (second == base), 1.0, 0.0)
            found = jnp.dot(held, onehot.astype(jnp.bfloat16), preferred_element_type=jnp.float32)
            for half in range(2):
                tile = found[:, LANES * half : LANES * (half + 1)]
                groups = tile[0:8], tile[8:16], tile[16:24]
                number = turn * 4 + half * 2
                store_block(out_ref, number, pack(*groups, 0))
                store_block(out_ref, number + 1, pack(*groups, PACK))


def run_turn(experts, h, back, rows, before, after):
    features, tokens = h.shape
    merge, send = before is not None, after is not None
    operands, specs, scratch = [h], [VMEM], []
    shapes, outs = [jax.ShapeDtypeStruct(h.shape, h.dtype)], [VMEM]
    if merge:
        operands += [back, rows]
        specs += [VMEM, plane((8, tokens), before)]
        scratch += [pltpu.VMEM((experts, 16, LANES), jnp.float32)]
    if send:
        operands += [rows]
        specs += [plane((8, tokens), after)]
        shapes += [jax.ShapeDtypeStruct((experts * TILES, 2, LANES), jnp.bfloat16)]
        outs += [VMEM]
    return pl.pallas_call(
        functools.partial(turn_kernel, merge, send),
        out_shape=tuple(shapes),
        grid=(1,),
        in_specs=specs,
        out_specs=tuple(outs),
        scratch_shapes=scratch,
        compiler_params=pltpu.CompilerParams(vmem_limit_bytes=VMEM_LIMIT),
        name="turn",
    )(*operands)


def expert_kernel(
    scal_ref, blocks_ref, gain_ref, router_ref, lane_ref, other_ref, out_ref,
    win_ref, wout_ref, wide_ref, sems,
):
    core = scal_ref[0]

    @pl.when(core == 0)
    def _():
        pltpu.make_async_copy(lane_ref, win_ref, sems.at[0]).start()
        pltpu.make_async_copy(other_ref, wout_ref, sems.at[1]).start()

    @pl.when(core != 0)
    def _():
        pltpu.make_async_copy(other_ref, win_ref, sems.at[0]).start()
        pltpu.make_async_copy(lane_ref, wout_ref, sems.at[1]).start()

    width = win_ref.shape[1]
    groups = wide_ref.shape[0]
    blocks = load_blocks(blocks_ref, wide_ref)
    parts = [group[:, None] for group in unpack(blocks, 0)[0:3]]
    tall = jnp.concatenate(parts, axis=1).reshape(width, LANES)
    wide = tall.T[0:PACK]
    mean_square = jnp.mean(wide * wide, axis=1, keepdims=True)
    normed = (wide * lax.rsqrt(mean_square + 1e-06) * gain_ref[...]).astype(jnp.bfloat16)
    logit = jnp.sum(normed.astype(jnp.float32) * router_ref[...], axis=1, keepdims=True)
    gate = jax.nn.sigmoid(logit).astype(jnp.bfloat16).astype(jnp.float32)
    pltpu.make_async_copy(lane_ref, win_ref, sems.at[0]).wait()
    pre_act = lax.dot_general(
        normed, win_ref[...], (((1,), (1,)), ((), ())), preferred_element_type=jnp.float32
    )
    active = jax.nn.gelu(pre_act, approximate=True).astype(jnp.bfloat16)
    pltpu.make_async_copy(lane_ref, wout_ref, sems.at[1]).wait()
    output = jnp.dot(active, wout_ref[...], preferred_element_type=jnp.float32)
    weighted = output * gate
    spread = jnp.broadcast_to(gate, (PACK, LANES))
    zeros = jnp.zeros_like(weighted)
    tall = jnp.concatenate([weighted, zeros], axis=0).T.reshape(groups, 3, 8, LANES)
    gates = jnp.concatenate([spread, jnp.zeros_like(spread)], axis=0).T[0:8]
    gates = jnp.broadcast_to(gates[None], (groups, 8, LANES))
    packed = pack(tall[:, 0], tall[:, 1], tall[:, 2], 0, gates)
    for number in range(groups):
        store_block(out_ref, number, packed[number])


def run_expert(layer, scal, blocks, gains, routers, lane_w, other_w):
    hidden, width = lane_w.shape
    return pl.pallas_call(
        expert_kernel,
        out_shape=jax.ShapeDtypeStruct(blocks.shape, jnp.bfloat16),
        grid=(1,),
        in_specs=[SMEM, VMEM, plane((1, width), layer), plane((1, width), layer), HBM, HBM],
        out_specs=VMEM,
        scratch_shapes=[
            pltpu.VMEM((hidden, width), jnp.bfloat16),
            pltpu.VMEM((hidden, width), jnp.bfloat16),
            pltpu.VMEM((blocks.shape[0] // TILES, 16, LANES), jnp.float32),
            pltpu.SemaphoreType.DMA((2,)),
        ],
        compiler_params=pltpu.CompilerParams(vmem_limit_bytes=VMEM_LIMIT),
        cost_estimate=pl.CostEstimate(
            flops=4 * PACK * hidden * width, bytes_accessed=4 * hidden * width, transcendentals=0
        ),
        name="expert",
    )(scal, blocks, gains, routers, lane_w, other_w)


def plane(shape, *lead):
    return pl.BlockSpec((None,) * len(lead) + shape, lambda i: lead + (0,) * len(shape))


def place_tokens(routes, experts):
    tokens = routes.shape[1]
    ids = jnp.arange(experts, dtype=jnp.int32)
    first = routes[:, :, 0:1] == ids
    second = routes[:, :, 1:2] == ids
    named = (first | second).astype(jnp.bfloat16)
    earlier = jnp.tril(jnp.ones((tokens, tokens), jnp.bfloat16), -1)
    rank = jnp.einsum("ut,lte->lue", earlier, named, preferred_element_type=jnp.float32)
    rank = rank.astype(jnp.int32) + ids * PACK
    slot_first = jnp.sum(jnp.where(first, rank, 0), axis=2)
    slot_second = jnp.sum(jnp.where(second, rank, 0), axis=2)
    blank = jnp.zeros_like(slot_first)
    return jnp.stack([slot_first, slot_second] + [blank] * 6, axis=1)


def join(*values):
    return lax.optimization_barrier(values)


def local(inputs, routes, norm_gains, routers, expert_in, expert_out):
    sections = lax.axis_size("section")
    experts = lax.axis_size("expert")
    section_pos = lax.axis_index("section")
    repeats, _, _, hidden, width = expert_in.shape
    layers = repeats * sections
    steps, held = ring_plan(sections, layers, PARTS, LEAD)
    size = hidden // PARTS
    scal = jnp.stack([section_pos % 2, section_pos]).astype(jnp.int32)

    buffers = {("in", r): (expert_in, (r, 0, 0)) for r in range(repeats)}
    buffers.update({("out", r): (expert_out, (r, 0, 0)) for r in range(repeats)})
    every = [(lane, y) for lane in range(2) for y in range(sections // 2)]
    table, wanted = [], []

    def source_of(lane, y, i):
        q, part = i // PARTS, i % PARTS
        if q % sections // 2 != y:
            _, number, place = held[lane][y][i]
            return ("ring", number), place * size
        name = ("in", "out")[lane] if q % 2 == lane else "swapped"
        return (name, q // sections), part * size

    def add_pick(by_section):
        choices = sorted(set(by_section.values()))
        table.append([choices.index(by_section.get(s, choices[0])) for s in range(sections)])
        wanted.append(choices)
        return len(table) - 1

    swap_rows = [
        [
            add_pick({2 * y + lane: ((("out", "in")[lane], r), part * size) for lane, y in every})
            for part in range(PARTS)
        ]
        for r in range(repeats)
    ]
    ring_rows = [
        [
            add_pick({2 * y + lane: source_of(lane, y, i) for lane, y, _, i, at in moves if at == place})
            for place in sorted({move[4] for move in moves})
        ]
        for moves in steps
    ]
    layer_rows = [
        [
            add_pick({2 * y + lane: source_of(lane, y, q * PARTS + part) for lane, y in every})
            for part in range(PARTS)
        ]
        for q in range(layers)
    ]
    tab = jnp.asarray(np.array(table, np.int32).T)[section_pos]

    def picked(rows, tab):
        names = sorted({name for row in rows for name, _ in wanted[row]})
        found = [buffers[name] for name in names]
        plan = tuple(
            (row, tuple((names.index(name), start) for name, start in wanted[row])) for row in rows
        )
        places = [place for _, place in found]
        return pick(tab, plan, [array for array, _ in found], places, size, width)

    def swapped(value):
        return lax.ppermute(value, "section", [(s, s ^ 1) for s in range(sections)])

    def ring(number, tab):
        if number > len(steps):
            return None
        moves = steps[number - 1]
        pairs = sorted({(2 * y + lane, 2 * target + lane) for lane, y, target, _, _ in moves})
        return lax.ppermute(picked(ring_rows[number - 1], tab), "section", pairs)

    def arrival(q):
        parts = range(q * PARTS, (q + 1) * PARTS)
        return max(stock[i][0] for lane in held for stock in lane for i in parts)

    mine = lax.all_to_all(routes[:, 0], "section", split_axis=1, concat_axis=0, tiled=False)
    mine = jnp.transpose(mine, (1, 0, 2, 3)).reshape(layers, -1, 2)
    rows = place_tokens(mine, experts)
    small = jnp.stack([norm_gains[:, 0], routers[:, 0, 0]])
    small = jnp.broadcast_to(small[None], (sections,) + small.shape)
    small = lax.all_to_all(small, "section", split_axis=0, concat_axis=0, tiled=True)
    small = jnp.transpose(small, (1, 2, 0, 3)).reshape(2, layers, 1, width).astype(jnp.float32)
    gains, gate_rows = small[0], small[1]
    h = jnp.transpose(inputs[0], (1, 0))

    buffers[("swapped", 0)] = (swapped(picked(swap_rows[0], tab)), ())
    later = swapped(picked(swap_rows[1], tab))
    flying = None
    for number in range(1, LEAD + 1):
        started = ring(number, tab)
        if flying is not None:
            flying, tab = join(flying, tab)
            buffers[("ring", number - 1)] = (flying, ())
        if number == 2:
            later, tab = join(later, tab)
            buffers[("swapped", 1)] = (later, ())
        flying = started
    flying, tab, rows, gains, gate_rows, h = join(flying, tab, rows, gains, gate_rows, h)
    buffers[("ring", LEAD)] = (flying, ())

    back = coming = None
    for q in range(layers):
        h, blocks = run_turn(experts, h, back, rows, q - 1 if q else None, q)
        blocks, tab = join(blocks, tab)
        sent = send_blocks(blocks)
        flying = ring(LEAD + 1 + q, tab)
        if coming is None:
            lane_w = picked(layer_rows[q], tab)
            coming = (lane_w, swapped(lane_w))
        blocks, lane_w, other_w, tab = join(sent, *coming, tab)
        back = run_expert(q, scal, blocks, gains, gate_rows, lane_w, other_w)
        back, tab = join(back, tab)
        sent = send_blocks(back)
        coming = None
        if q + 1 < layers and arrival(q + 1) < LEAD + 1 + q:
            lane_w = picked(layer_rows[q + 1], tab)
            coming = (lane_w, swapped(lane_w))
        if flying is None:
            back, tab = join(sent, tab)
        else:
            back, flying, tab = join(sent, flying, tab)
            buffers[("ring", LEAD + 1 + q)] = (flying, ())

    (h,) = run_turn(experts, h, back, rows, layers - 1, None)
    return jnp.transpose(h, (1, 0))[None]


def solution(mesh):
    return jax.shard_map(
        local,
        mesh=mesh,
        in_specs=(
            P("section", None, "expert"),
            P(None, "section", None, None, None),
            P(None, "section", None),
            P(None, "section", "expert", None),
            P(None, "section", "expert", None, None),
            P(None, "section", "expert", None, None),
        ),
        out_specs=P("section", None, "expert"),
        check_vma=False,
    )
```

```python
import functools

import jax
import jax.numpy as jnp
import numpy as np
from jax import lax
from jax.experimental import pallas as pl
from jax.experimental.pallas import tpu as pltpu
from jax.sharding import PartitionSpec as P

VMEM_LIMIT = 64400 * 1024
HBM = pl.BlockSpec(memory_space=pltpu.HBM)
SMEM = pl.BlockSpec(memory_space=pltpu.SMEM)
VMEM = pl.BlockSpec(memory_space=pltpu.VMEM)
DIRS = (1, -1)


PACK = 64
SLOTS = 48
ROWS = 10
PARTS = 2
UNROLL = 2
AHEAD = (64, 20, 1, 3, 1, 5, 6, 4, 4, 2, 4, 3, 6, 3, 2, 5)
AHEAD_A_HOP = (13.5, 49, 3.5, 0.5, 3.5, 0.5, 1.5, 0.5, 0.5, 0.5, 0.5, 0.5, 0.5, 1, 1, 0.5)
LEAD = 8


def ring_plan(sections, layers, parts, lead):
    chips = sections // 2
    items = layers * parts

    def earliest(i, lane, target):
        hops = ((i // parts) % sections // 2 - target) * DIRS[lane] % chips
        return lead + i // parts - AHEAD[i // parts] - AHEAD_A_HOP[i // parts] * hops

    held = [
        [
            {i: (0, 0, 0) for i in range(items) if (i // parts) % sections // 2 == y}
            for y in range(chips)
        ]
        for _ in DIRS
    ]
    steps = []
    while any(len(stock) < items for lane in held for stock in lane):
        number = len(steps) + 1
        moves = []
        for lane, step in enumerate(DIRS):
            for y in range(chips):
                target = (y + step) % chips
                there = held[lane][target]
                options = [i for i, at in held[lane][y].items() if at[0] < number and i not in there]
                options = sorted(i for i in options if number >= earliest(i, lane, target))
                for place, i in enumerate(options[: 1 if number <= lead else parts]):
                    moves.append((lane, y, target, i, place))
        steps.append(moves)
        for lane, _, target, i, place in moves:
            held[lane][target][i] = (number + (number < lead), number, place)
    return steps, held


class Reads:
    def __init__(self, rows, places, size, tab_ref, sources, hold_ref, sems):
        self.rows, self.places, self.size = rows, places, size
        self.tab_ref, self.sources = tab_ref, sources
        self.hold_ref, self.sems = hold_ref, sems

    def part_of(self, ref, part):
        return ref.at[pl.ds(pl.multiple_of(part * self.size, self.size), self.size)]

    def copy(self, part, choice):
        number, start = choice
        view = self.sources[number].at[self.places[number] + (pl.ds(start, self.size),)]
        return pltpu.make_async_copy(view, self.part_of(self.hold_ref, part), self.sems.at[part])

    def start(self):
        for part, (row, choices) in enumerate(self.rows):
            wish = self.tab_ref[row]
            for number, choice in enumerate(choices):

                @pl.when(wish == number)
                def _(part=part, choice=choice):
                    self.copy(part, choice).start()

    def wait(self, part):
        to = self.part_of(self.hold_ref, part)
        pltpu.make_async_copy(to, to, self.sems.at[part]).wait()

    def forward(self, out_ref, sems):
        for part in range(len(self.rows)):
            self.wait(part)
            self.leave(part, out_ref, sems).start()

    def finish(self, out_ref, sems):
        for part in range(len(self.rows)):
            self.leave(part, out_ref, sems).wait()

    def leave(self, part, out_ref, sems):
        return pltpu.make_async_copy(
            self.part_of(self.hold_ref, part), self.part_of(out_ref, part), sems.at[part]
        )


def pick_kernel(rows, places, size, tab_ref, *refs):
    count = len(places)
    sources, (out_ref, hold_ref, in_sems, out_sems) = refs[:count], refs[count:]
    reads = Reads(rows, places, size, tab_ref, sources, hold_ref, in_sems)
    reads.start()
    reads.forward(out_ref, out_sems)
    reads.finish(out_ref, out_sems)


def pick(tab, rows, sources, places, size, width):
    shape = (size * len(rows), width)
    return pl.pallas_call(
        functools.partial(pick_kernel, rows, places, size),
        out_shape=jax.ShapeDtypeStruct(shape, jnp.bfloat16),
        in_specs=[SMEM] + [HBM] * len(sources),
        out_specs=HBM,
        scratch_shapes=[
            pltpu.VMEM(shape, jnp.bfloat16),
            pltpu.SemaphoreType.DMA((len(rows),)),
            pltpu.SemaphoreType.DMA((len(rows),)),
        ],
        compiler_params=pltpu.CompilerParams(vmem_limit_bytes=VMEM_LIMIT),
        cost_estimate=pl.CostEstimate(
            flops=0, bytes_accessed=4 * shape[0] * width, transcendentals=0
        ),
        name="pick",
    )(tab, *sources)


LANES = 128


def turned(value, lanes):
    return pltpu.roll(value, lanes % LANES, value.ndim - 1)


def lanes_of(value):
    return lax.broadcasted_iota(jnp.int32, (1,) * (value.ndim - 1) + (LANES,), value.ndim - 1)


def fold_tail(third, at):
    axis = third.ndim - 1
    spread = pltpu.roll(turned(third, -at - 32), 0, axis, stride=16, stride_axis=axis - 1)
    place = lax.broadcasted_iota(jnp.int32, third.shape, axis) // 16
    own = place == lax.broadcasted_iota(jnp.int32, third.shape, axis - 1)
    return jnp.sum(jnp.where(own, spread, 0.0), axis=axis - 1, keepdims=True)


def unfold_tail(row, at):
    value = jnp.broadcast_to(turned(row, at + 32), row.shape[:-2] + (8, LANES))
    number = lax.broadcasted_iota(jnp.int32, value.shape, value.ndim - 2)
    for step in (1, 2, 4):
        value = jnp.where((number & step) != 0, turned(value, -16 * step), value)
    return value


def pack(first, second, third, at, gates=None):
    lanes = lanes_of(first)
    top = jnp.where(
        lanes < SLOTS,
        turned(first, -at),
        jnp.where(lanes < 2 * SLOTS, turned(second, SLOTS - at), turned(third, 2 * SLOTS - at)),
    )
    tail = fold_tail(third, at)
    axis = first.ndim - 2
    number = lax.broadcasted_iota(jnp.int32, top.shape, axis)
    last = jnp.broadcast_to(tail, top.shape)
    if gates is not None:
        last = jnp.where(number == 0, last, gates)
    return jnp.concatenate([top, last], axis=axis)


def unpack(blocks, at):
    top, last = blocks[..., 0:8, :], blocks[..., 8:16, :]
    lanes = lanes_of(blocks)
    third = jnp.where(
        lanes - at < 32, turned(top, at - 2 * SLOTS), unfold_tail(last[..., 0:1, :], at)
    )
    return turned(top, at), turned(top, at - SLOTS), third, turned(last, at)


def unpack_pairs(back):
    pairs = back.shape[0] // 2
    split = back.reshape(pairs, 2, 16, LANES)
    low = lanes_of(back) < PACK
    both = zip(unpack(split[:, 0], 0), unpack(split[:, 1], PACK))
    groups = [jnp.where(low, even, odd) for even, odd in both]
    gates = jnp.broadcast_to(groups[3][:, 1:2], groups[0].shape)
    return jnp.concatenate(groups[0:3] + [gates], axis=1)


TILES = ROWS // 2


def load_blocks(ref, wide_ref):
    @pl.loop(0, wide_ref.shape[0], step=8)
    def _(begin):
        for more in range(8):
            block = ref[pl.ds(TILES * (begin + more), TILES)].reshape(ROWS, LANES)
            wide_ref[begin + more, 0:ROWS] = block.astype(jnp.float32)

    return wide_ref[...]


def store_block(ref, number, block):
    rows = block.astype(jnp.bfloat16).reshape(8, 2, LANES)
    ref[pl.ds(TILES * number, TILES)] = rows[0:TILES]


def send_blocks(value):
    return lax.all_to_all(value, "expert", split_axis=0, concat_axis=0, tiled=True)


def turn_kernel(merge, send, side, *refs):
    refs = list(refs)
    h_ref = refs.pop(0)
    if merge:
        back_ref, row_ref = refs.pop(0), refs.pop(0)
    if send:
        next_ref = refs.pop(0)
    if side:
        (rows, places, size), count = side, len(side[1])
        out_sems, in_sems, hold_ref = refs.pop(), refs.pop(), refs.pop()
        tab_ref, sources = refs.pop(0), refs[:count]
        del refs[:count]
        reads = Reads(rows, places, size, tab_ref, sources, hold_ref, in_sems)
        reads.start()
    if merge:
        tiles_ref, update_ref, wide_ref = refs.pop(), refs.pop(), refs.pop()
    hnew_ref = refs.pop(0)
    features, tokens = h_ref.shape
    held = h_ref[...]
    if merge:
        tiles = unpack_pairs(load_blocks(back_ref, wide_ref)).astype(jnp.bfloat16)
        offset = lax.broadcasted_iota(jnp.int32, (4 * PACK, tokens), 0)
        first, second = row_ref[0:1, :] - offset, row_ref[1:2, :] - offset
        tiles_ref[...] = tiles
        update_ref[...] = jnp.zeros_like(update_ref)

        @pl.loop(0, tiles.shape[0] // 2, step=4)
        def _(begin):
            update = update_ref[...]
            for more in range(4):
                turn = begin + more
                base = turn * 4 * PACK
                onehot = jnp.where((first == base) | (second == base), 1.0, 0.0)
                pair = jnp.concatenate([tiles_ref[2 * turn], tiles_ref[2 * turn + 1]], axis=1)
                update += jnp.dot(
                    pair, onehot.astype(jnp.bfloat16), preferred_element_type=jnp.float32
                )
            update_ref[...] = update

        update = update_ref[...]
        change = update[0:features] * (1.0 / update[features:features + 1])
        held = (held.astype(jnp.float32) + change).astype(jnp.bfloat16)
    hnew_ref[...] = held
    if send:
        out_ref = refs.pop(0)
    if side:
        side_ref = refs.pop(0)
        reads.forward(side_ref, out_sems)
    if send:
        offset = lax.broadcasted_iota(jnp.int32, (tokens, 4 * PACK), 1)
        col = next_ref[...].astype(jnp.float32).T.astype(jnp.int32)
        first, second = col[:, 0:1] - offset, col[:, 1:2] - offset
        @pl.loop(0, out_ref.shape[0] // TILES // 4, step=UNROLL)
        def _(begin):
            for more in range(UNROLL):
                turn = begin + more
                base = turn * 4 * PACK
                onehot = jnp.where((first == base) | (second == base), 1.0, 0.0)
                found = jnp.dot(held, onehot.astype(jnp.bfloat16), preferred_element_type=jnp.float32)
                for half in range(2):
                    tile = found[:, LANES * half : LANES * (half + 1)]
                    groups = tile[0:8], tile[8:16], tile[16:24]
                    number = turn * 4 + half * 2
                    store_block(out_ref, number, pack(*groups, 0))
                    store_block(out_ref, number + 1, pack(*groups, PACK))
    if side:
        reads.finish(side_ref, out_sems)


def run_turn(experts, h, back, rows, before, after, side=None):
    features, tokens = h.shape
    merge, send = before is not None, after is not None
    operands, specs, scratch = [h], [VMEM], []
    shapes, outs = [jax.ShapeDtypeStruct(h.shape, h.dtype)], [VMEM]
    if merge:
        operands += [back, rows]
        specs += [VMEM, plane((8, tokens), before)]
        scratch += [
            pltpu.VMEM((experts, 16, LANES), jnp.float32),
            pltpu.VMEM((32, tokens), jnp.float32),
            pltpu.VMEM((experts // 2, 32, LANES), jnp.bfloat16),
        ]
    if send:
        operands += [rows]
        specs += [plane((8, tokens), after)]
        shapes += [jax.ShapeDtypeStruct((experts * TILES, 2, LANES), jnp.bfloat16)]
        outs += [VMEM]
    plan = None
    if side is not None:
        tab, picks, sources, places, size, width = side
        plan = (picks, places, size)
        operands += [tab] + sources
        specs += [SMEM] + [HBM] * len(sources)
        shape = (size * len(picks), width)
        shapes += [jax.ShapeDtypeStruct(shape, jnp.bfloat16)]
        outs += [HBM]
        scratch += [
            pltpu.VMEM(shape, jnp.bfloat16),
            pltpu.SemaphoreType.DMA((len(picks),)),
            pltpu.SemaphoreType.DMA((len(picks),)),
        ]
    return pl.pallas_call(
        functools.partial(turn_kernel, merge, send, plan),
        out_shape=tuple(shapes),
        grid=(1,),
        in_specs=specs,
        out_specs=tuple(outs),
        scratch_shapes=scratch,
        compiler_params=pltpu.CompilerParams(vmem_limit_bytes=VMEM_LIMIT),
        name="turn",
    )(*operands)


def expert_kernel(in_rows, out_rows, places, size, blocks_ref, gain_ref, router_ref, tab_ref, *refs):
    sources, refs = refs[: len(places)], refs[len(places) :]
    out_ref, win_ref, wout_ref, wide_ref, sum_ref, in_sems, out_sems = refs
    in_reads = Reads(in_rows, places, size, tab_ref, sources, win_ref, in_sems)
    out_reads = Reads(out_rows, places, size, tab_ref, sources, wout_ref, out_sems)
    in_reads.start()
    out_reads.start()
    width = win_ref.shape[1]
    groups = wide_ref.shape[0]
    blocks = load_blocks(blocks_ref, wide_ref)
    parts = [group[:, None] for group in unpack(blocks, 0)[0:3]]
    tall = jnp.concatenate(parts, axis=1).reshape(width, LANES)
    wide = tall.T[0:PACK]
    mean_square = jnp.mean(wide * wide, axis=1, keepdims=True)
    normed = (wide * lax.rsqrt(mean_square + 1e-06) * gain_ref[...]).astype(jnp.bfloat16)
    logit = jnp.sum(normed.astype(jnp.float32) * router_ref[...], axis=1, keepdims=True)
    gate = jax.nn.sigmoid(logit).astype(jnp.bfloat16).astype(jnp.float32)
    sum_ref[...] = jnp.zeros_like(sum_ref)

    @pl.loop(0, len(in_rows))
    def _(part):
        some = pl.ds(pl.multiple_of(part * size, size), size)
        in_reads.wait(part)
        pre_act = lax.dot_general(
            normed, win_ref[some], (((1,), (1,)), ((), ())), preferred_element_type=jnp.float32
        )
        active = jax.nn.gelu(pre_act, approximate=True).astype(jnp.bfloat16)
        out_reads.wait(part)
        sum_ref[...] += jnp.dot(active, wout_ref[some], preferred_element_type=jnp.float32)

    output = sum_ref[...]
    weighted = output * gate
    spread = jnp.broadcast_to(gate, (PACK, LANES))
    zeros = jnp.zeros_like(weighted)
    tall = jnp.concatenate([weighted, zeros], axis=0).T.reshape(groups, 3, 8, LANES)
    gates = jnp.concatenate([spread, jnp.zeros_like(spread)], axis=0).T[0:8]
    gates = jnp.broadcast_to(gates[None], (groups, 8, LANES))
    packed = pack(tall[:, 0], tall[:, 1], tall[:, 2], 0, gates)
    wide_ref[...] = packed

    @pl.loop(0, groups, step=8)
    def _(begin):
        for more in range(8):
            store_block(out_ref, begin + more, wide_ref[begin + more])


def run_expert(layer, blocks, gains, routers, weights):
    tab, (in_rows, out_rows), sources, places, size, width = weights
    hidden = size * len(in_rows)
    return pl.pallas_call(
        functools.partial(expert_kernel, in_rows, out_rows, places, size),
        out_shape=jax.ShapeDtypeStruct(blocks.shape, jnp.bfloat16),
        grid=(1,),
        in_specs=[VMEM, plane((1, width), layer), plane((1, width), layer), SMEM]
        + [HBM] * len(sources),
        out_specs=VMEM,
        scratch_shapes=[
            pltpu.VMEM((hidden, width), jnp.bfloat16),
            pltpu.VMEM((hidden, width), jnp.bfloat16),
            pltpu.VMEM((blocks.shape[0] // TILES, 16, LANES), jnp.float32),
            pltpu.VMEM((PACK, width), jnp.float32),
            pltpu.SemaphoreType.DMA((len(in_rows),)),
            pltpu.SemaphoreType.DMA((len(out_rows),)),
        ],
        compiler_params=pltpu.CompilerParams(vmem_limit_bytes=VMEM_LIMIT),
        cost_estimate=pl.CostEstimate(
            flops=4 * PACK * hidden * width, bytes_accessed=4 * hidden * width, transcendentals=0
        ),
        name="expert",
    )(blocks, gains, routers, tab, *sources)


def plane(shape, *lead):
    return pl.BlockSpec((None,) * len(lead) + shape, lambda i: lead + (0,) * len(shape))


def place_tokens(routes, experts):
    tokens = routes.shape[1]
    ids = jnp.arange(experts, dtype=jnp.int32)
    first = routes[:, :, 0:1] == ids
    second = routes[:, :, 1:2] == ids
    named = (first | second).astype(jnp.bfloat16)
    earlier = jnp.tril(jnp.ones((tokens, tokens), jnp.bfloat16), -1)
    rank = jnp.einsum("ut,lte->lue", earlier, named, preferred_element_type=jnp.float32)
    rank = rank.astype(jnp.int32) + ids * PACK
    slot_first = jnp.sum(jnp.where(first, rank, 0), axis=2)
    slot_second = jnp.sum(jnp.where(second, rank, 0), axis=2)
    blank = jnp.zeros_like(slot_first)
    return jnp.stack([slot_first, slot_second] + [blank] * 6, axis=1)


def join(*values):
    return lax.optimization_barrier(values)


def local(inputs, routes, norm_gains, routers, expert_in, expert_out):
    sections = lax.axis_size("section")
    experts = lax.axis_size("expert")
    section_pos = lax.axis_index("section")
    repeats, _, _, hidden, width = expert_in.shape
    layers = repeats * sections
    steps, held = ring_plan(sections, layers, PARTS, LEAD)
    size = hidden // PARTS

    buffers = {("in", r): (expert_in, (r, 0, 0)) for r in range(repeats)}
    buffers.update({("out", r): (expert_out, (r, 0, 0)) for r in range(repeats)})
    every = [(lane, y) for lane in range(2) for y in range(sections // 2)]
    table, wanted = [], []

    def source_of(lane, y, i):
        q, part = i // PARTS, i % PARTS
        if q % sections // 2 != y:
            _, number, place = held[lane][y][i]
            return ("ring", number), place * size
        name = ("in", "out")[lane] if q % 2 == lane else "swapped"
        return (name, q // sections), part * size

    def other_of(lane, y, i):
        q, part = i // PARTS, i % PARTS
        if q % sections // 2 != y:
            _, number, place = held[1 - lane][y][i]
            return ("turned", number), place * size
        name = ("out", "in")[lane] if q % 2 == lane else "given"
        return (name, q // sections), part * size

    def add_pick(by_section):
        choices = sorted(set(by_section.values()))
        table.append([choices.index(by_section.get(s, choices[0])) for s in range(sections)])
        wanted.append(choices)
        return len(table) - 1

    swap_rows = [
        [
            add_pick({2 * y + lane: ((("out", "in")[lane], r), part * size) for lane, y in every})
            for part in range(PARTS)
        ]
        for r in range(repeats)
    ]
    ring_rows = [
        [
            add_pick({2 * y + lane: source_of(lane, y, i) for lane, y, _, i, at in moves if at == place})
            for place in sorted({move[4] for move in moves})
        ]
        for moves in steps
    ]
    give_rows = [
        [
            add_pick({2 * y + lane: ((("in", "out")[lane], r), part * size) for lane, y in every})
            for part in range(PARTS)
        ]
        for r in range(repeats)
    ]

    def matrix_rows(q, kind):
        found = []
        for part in range(PARTS):
            i = q * PARTS + part
            by_section = {
                2 * y + lane: (source_of if lane == kind else other_of)(lane, y, i)
                for lane, y in every
            }
            found.append(add_pick(by_section))
        return found

    layer_rows = [(matrix_rows(q, 0), matrix_rows(q, 1)) for q in range(layers)]
    tab = jnp.asarray(np.array(table, np.int32).T)[section_pos]

    def plan_of(groups, tab):
        names = sorted({name for rows in groups for row in rows for name, _ in wanted[row]})
        found = [buffers[name] for name in names]
        plans = [
            tuple(
                (row, tuple((names.index(name), start) for name, start in wanted[row]))
                for row in rows
            )
            for rows in groups
        ]
        arrays, places = [array for array, _ in found], [place for _, place in found]
        return tab, plans, arrays, places, size, width

    def picked(rows, tab):
        tab, (plan,), arrays, places, size, width = plan_of([rows], tab)
        return pick(tab, plan, arrays, places, size, width)

    def swapped(value):
        return lax.ppermute(value, "section", [(s, s ^ 1) for s in range(sections)])

    def ring(number, value):
        moves = steps[number - 1]
        pairs = sorted({(2 * y + lane, 2 * target + lane) for lane, y, target, _, _ in moves})
        return lax.ppermute(value, "section", pairs)

    def arrived(number, value):
        buffers[("ring", number)] = (value, ())

    def turned_over(number):
        return swapped(buffers[("ring", number)][0])

    over_at = {q: [] for q in range(layers)}
    for number in range(LEAD - 1, len(steps) + 1):
        users = [
            i // PARTS for lane in held for stock in lane for i, at in stock.items() if at[1] == number
        ]
        over_at[max(min(users), number + 1 - LEAD, 1)].append(number)
    first_later = min(
        number
        for number, rows in enumerate(ring_rows, 1)
        for row in rows
        if ("swapped", 1) in {name for name, _ in wanted[row]}
    )
    own_at = {max(first_later - 1 - LEAD, 1): ("swapped", swap_rows), sections - 1: ("given", give_rows)}

    mine = lax.all_to_all(routes[:, 0], "section", split_axis=1, concat_axis=0, tiled=False)
    mine = jnp.transpose(mine, (1, 0, 2, 3)).reshape(layers, -1, 2)
    rows = place_tokens(mine, experts)
    small = jnp.stack([norm_gains[:, 0], routers[:, 0, 0]])
    small = jnp.broadcast_to(small[None], (sections,) + small.shape)
    small = lax.all_to_all(small, "section", split_axis=0, concat_axis=0, tiled=True)
    small = jnp.transpose(small, (1, 2, 0, 3)).reshape(2, layers, 1, width).astype(jnp.float32)
    gains, gate_rows = small[0], small[1]
    h = jnp.transpose(inputs[0], (1, 0))

    buffers[("swapped", 0)] = (swapped(picked(swap_rows[0], tab)), ())
    flying = waiting = None
    for number in range(1, LEAD + 1):
        started = ring(number, picked(ring_rows[number - 1], tab))
        if number == 1:
            given = swapped(picked(give_rows[0], tab))
        if number == 2:
            given, tab, rows, gains, gate_rows, h = join(given, tab, rows, gains, gate_rows, h)
            buffers[("given", 0)] = (given, ())
        if number == 3:
            h, blocks = run_turn(experts, h, None, rows, None, 0)
            blocks, tab = join(blocks, tab)
            blocks = send_blocks(blocks)
        if waiting is not None:
            waiting, tab = join(waiting, tab)
            buffers[("turned", number - 2)] = (waiting, ())
        if flying is not None and number < LEAD:
            flying, tab = join(flying, tab)
            arrived(number - 1, flying)
            waiting = turned_over(number - 1)
        if number == 5:
            blocks, tab = join(blocks, tab)
        if number < LEAD:
            flying = started
    under_way = [flying, started]

    for q in range(layers):
        number = LEAD + q
        if q:
            side = None
            if number <= len(steps):
                tab, (plan,), *place = plan_of([ring_rows[number - 1]], tab)
                side = (tab, plan, *place)
            h, blocks, *extra = run_turn(experts, h, back, rows, q - 1, q, side)
            blocks, tab = join(blocks, tab)
            sent = send_blocks(blocks)
            under_way = [ring(number, extra[0])] if extra else []
            swaps = {("turned", n): turned_over(n) for n in over_at[q]}
            if q in own_at:
                name, some = own_at[q]
                swaps[(name, 1)] = swapped(picked(some[1], tab))
            blocks, tab, *values = join(sent, tab, *swaps.values())
            buffers.update({name: (value, ()) for name, value in zip(swaps, values)})
        back = run_expert(q, blocks, gains, gate_rows, plan_of(layer_rows[q], tab))
        back, tab, *under_way = join(send_blocks(back), tab, *under_way)
        for back_by, value in enumerate(reversed(under_way)):
            arrived(number - back_by, value)

    (h,) = run_turn(experts, h, back, rows, layers - 1, None)
    return jnp.transpose(h, (1, 0))[None]


def solution(mesh):
    return jax.shard_map(
        local,
        mesh=mesh,
        in_specs=(
            P("section", None, "expert"),
            P(None, "section", None, None, None),
            P(None, "section", None),
            P(None, "section", "expert", None),
            P(None, "section", "expert", None, None),
            P(None, "section", "expert", None, None),
        ),
        out_specs=P("section", None, "expert"),
        check_vma=False,
    )
```

```python
import functools

import jax
import jax.numpy as jnp
import numpy as np
from jax import lax
from jax.experimental import pallas as pl
from jax.experimental.pallas import tpu as pltpu
from jax.sharding import PartitionSpec as P

VMEM_LIMIT = 64400 * 1024
HBM = pl.BlockSpec(memory_space=pltpu.HBM)
SMEM = pl.BlockSpec(memory_space=pltpu.SMEM)
VMEM = pl.BlockSpec(memory_space=pltpu.VMEM)
DIRS = (1, -1)


PACK = 64
SLOTS = 48
ROWS = 10
PARTS = 2
LEAD = 6


def ring_plan(sections, layers, parts, lead):
    chips = sections // 2
    items = layers * parts
    held = [
        [
            {i: (0, 0, 0) for i in range(items) if (i // parts) % sections // 2 == y}
            for y in range(chips)
        ]
        for _ in DIRS
    ]
    steps = []
    while any(len(stock) < items for lane in held for stock in lane):
        number = len(steps) + 1
        moves = []
        for lane, step in enumerate(DIRS):
            for y in range(chips):
                target = (y + step) % chips
                there = held[lane][target]
                options = sorted(i for i, at in held[lane][y].items() if at[0] < number and i not in there)
                for place, i in enumerate(options[: 1 if number <= lead else parts]):
                    moves.append((lane, y, target, i, place))
        steps.append(moves)
        for lane, _, target, i, place in moves:
            held[lane][target][i] = (number + (number < lead), number, place)
    return steps, held


class Reads:
    def __init__(self, rows, places, size, tab_ref, sources, hold_ref, sems):
        self.rows, self.places, self.size = rows, places, size
        self.tab_ref, self.sources = tab_ref, sources
        self.hold_ref, self.sems = hold_ref, sems

    def part_of(self, ref, part):
        return ref.at[pl.ds(pl.multiple_of(part * self.size, self.size), self.size)]

    def copy(self, part, choice):
        number, start = choice
        view = self.sources[number].at[self.places[number] + (pl.ds(start, self.size),)]
        return pltpu.make_async_copy(view, self.part_of(self.hold_ref, part), self.sems.at[part])

    def start(self):
        for part, (row, choices) in enumerate(self.rows):
            wish = self.tab_ref[row]
            for number, choice in enumerate(choices):

                @pl.when(wish == number)
                def _(part=part, choice=choice):
                    self.copy(part, choice).start()

    def wait(self, part):
        to = self.part_of(self.hold_ref, part)
        pltpu.make_async_copy(to, to, self.sems.at[part]).wait()

    def forward(self, out_ref, sems):
        for part in range(len(self.rows)):
            self.wait(part)
            self.leave(part, out_ref, sems).start()

    def finish(self, out_ref, sems):
        for part in range(len(self.rows)):
            self.leave(part, out_ref, sems).wait()

    def leave(self, part, out_ref, sems):
        return pltpu.make_async_copy(
            self.part_of(self.hold_ref, part), self.part_of(out_ref, part), sems.at[part]
        )


class Side:
    def __init__(self, side):
        self.tab, self.jobs, arrays, self.places, self.size, width = side
        self.operands = [self.tab] + arrays
        self.in_specs = [SMEM] + [HBM] * len(arrays)
        shapes = [(self.size * len(rows), width) for rows in self.jobs]
        self.out_shapes = [jax.ShapeDtypeStruct(shape, jnp.bfloat16) for shape in shapes]
        self.out_specs = [HBM] * len(self.jobs)
        self.scratch = []
        for rows, shape in zip(self.jobs, shapes):
            self.scratch += [pltpu.VMEM(shape, jnp.bfloat16)]
            self.scratch += [pltpu.SemaphoreType.DMA((len(rows),))] * 2

    def bind(self, inputs, outputs, scratch):
        self.outputs = outputs
        self.reads = [
            Reads(rows, self.places, self.size, inputs[0], inputs[1:], hold_ref, in_sems)
            for rows, hold_ref, in_sems in zip(self.jobs, scratch[0::3], scratch[1::3])
        ]
        self.out_sems = scratch[2::3]

    def start(self):
        for reads in self.reads:
            reads.start()

    def forward(self):
        for reads, out_ref, sems in zip(self.reads, self.outputs, self.out_sems):
            reads.forward(out_ref, sems)

    def finish(self):
        for reads, out_ref, sems in zip(self.reads, self.outputs, self.out_sems):
            reads.finish(out_ref, sems)


def call_with_side(kernel, side, operands, in_specs, shapes, out_specs, scratch, **options):
    beside = Side(side)
    counts = [len(operands), len(beside.operands), len(shapes), len(beside.out_shapes), len(scratch)]

    def body(*refs):
        cuts = np.cumsum(counts)
        groups = [refs[end - count : end] for count, end in zip(counts, cuts)]
        beside.bind(groups[1], groups[3], refs[cuts[-1] :])
        kernel(beside, *groups[0], *groups[2], *groups[4])

    return pl.pallas_call(
        body,
        out_shape=tuple(shapes) + tuple(beside.out_shapes),
        grid=(1,),
        in_specs=list(in_specs) + beside.in_specs,
        out_specs=tuple(out_specs) + tuple(beside.out_specs),
        scratch_shapes=list(scratch) + beside.scratch,
        compiler_params=pltpu.CompilerParams(vmem_limit_bytes=VMEM_LIMIT),
        **options,
    )(*operands, *beside.operands)


def copy_kernel(side):
    side.start()
    side.forward()
    side.finish()


def pick(side):
    return call_with_side(copy_kernel, side, [], [], [], [], [], name="pick")[0]


LANES = 128


def turned(value, lanes):
    return pltpu.roll(value, lanes % LANES, value.ndim - 1)


def lanes_of(value):
    return lax.broadcasted_iota(jnp.int32, (1,) * (value.ndim - 1) + (LANES,), value.ndim - 1)


def fold_tail(third, at):
    axis = third.ndim - 1
    spread = pltpu.roll(turned(third, -at - 32), 0, axis, stride=16, stride_axis=axis - 1)
    place = lax.broadcasted_iota(jnp.int32, third.shape, axis) // 16
    own = place == lax.broadcasted_iota(jnp.int32, third.shape, axis - 1)
    return jnp.sum(jnp.where(own, spread, 0.0), axis=axis - 1, keepdims=True)


def unfold_tail(row, at):
    value = jnp.broadcast_to(turned(row, at + 32), row.shape[:-2] + (8, LANES))
    number = lax.broadcasted_iota(jnp.int32, value.shape, value.ndim - 2)
    for step in (1, 2, 4):
        value = jnp.where((number & step) != 0, turned(value, -16 * step), value)
    return value


def pack(first, second, third, at, gates=None):
    lanes = lanes_of(first)
    top = jnp.where(
        lanes < SLOTS,
        turned(first, -at),
        jnp.where(lanes < 2 * SLOTS, turned(second, SLOTS - at), turned(third, 2 * SLOTS - at)),
    )
    tail = fold_tail(third, at)
    axis = first.ndim - 2
    number = lax.broadcasted_iota(jnp.int32, top.shape, axis)
    last = jnp.broadcast_to(tail, top.shape)
    if gates is not None:
        last = jnp.where(number == 0, last, gates)
    return jnp.concatenate([top, last], axis=axis)


def unpack(blocks, at):
    top, last = blocks[..., 0:8, :], blocks[..., 8:16, :]
    lanes = lanes_of(blocks)
    third = jnp.where(
        lanes - at < 32, turned(top, at - 2 * SLOTS), unfold_tail(last[..., 0:1, :], at)
    )
    return turned(top, at), turned(top, at - SLOTS), third, turned(last, at)


def unpack_pairs(back):
    pairs = back.shape[0] // 2
    split = back.reshape(pairs, 2, 16, LANES)
    low = lanes_of(back) < PACK
    both = zip(unpack(split[:, 0], 0), unpack(split[:, 1], PACK))
    groups = [jnp.where(low, even, odd) for even, odd in both]
    gates = jnp.broadcast_to(groups[3][:, 1:2], groups[0].shape)
    return jnp.concatenate(groups[0:3] + [gates], axis=1)


TILES = ROWS // 2


def load_blocks(ref, wide_ref):
    for number in range(wide_ref.shape[0]):
        block = ref[TILES * number : TILES * (number + 1)].reshape(ROWS, LANES)
        wide_ref[number, 0:ROWS] = block.astype(jnp.float32)
    return wide_ref[...]


def store_block(ref, number, block):
    rows = block.astype(jnp.bfloat16).reshape(8, 2, LANES)
    ref[TILES * number : TILES * (number + 1)] = rows[0:TILES]


def send_blocks(value):
    return lax.all_to_all(value, "expert", split_axis=0, concat_axis=0, tiled=True)


def turn_kernel(merge, send, side, *refs):
    side.start()
    refs = list(refs)
    h_ref = refs.pop(0)
    if merge:
        back_ref, row_ref = refs.pop(0), refs.pop(0)
    if send:
        next_ref = refs.pop(0)
    hnew_ref = refs.pop(0)
    features, tokens = h_ref.shape
    held = h_ref[...]
    if merge:
        tiles = unpack_pairs(load_blocks(back_ref, refs.pop())).astype(jnp.bfloat16)
        offset = lax.broadcasted_iota(jnp.int32, (4 * PACK, tokens), 0)
        first, second = row_ref[0:1, :] - offset, row_ref[1:2, :] - offset
        update = jnp.zeros((32, tokens), jnp.float32)
        for turn in range(tiles.shape[0] // 2):
            base = turn * 4 * PACK
            onehot = jnp.where((first == base) | (second == base), 1.0, 0.0)
            pair = jnp.concatenate([tiles[2 * turn], tiles[2 * turn + 1]], axis=1)
            update += jnp.dot(
                pair, onehot.astype(jnp.bfloat16), preferred_element_type=jnp.float32
            )
        change = update[0:features] * (1.0 / update[features:features + 1])
        held = (held.astype(jnp.float32) + change).astype(jnp.bfloat16)
    hnew_ref[...] = held
    side.forward()
    if send:
        out_ref = refs.pop(0)
        offset = lax.broadcasted_iota(jnp.int32, (tokens, 4 * PACK), 1)
        col = next_ref[...].astype(jnp.float32).T.astype(jnp.int32)
        first, second = col[:, 0:1] - offset, col[:, 1:2] - offset
        for turn in range(out_ref.shape[0] // TILES // 4):
            base = turn * 4 * PACK
            onehot = jnp.where((first == base) | (second == base), 1.0, 0.0)
            found = jnp.dot(held, onehot.astype(jnp.bfloat16), preferred_element_type=jnp.float32)
            for half in range(2):
                tile = found[:, LANES * half : LANES * (half + 1)]
                groups = tile[0:8], tile[8:16], tile[16:24]
                number = turn * 4 + half * 2
                store_block(out_ref, number, pack(*groups, 0))
                store_block(out_ref, number + 1, pack(*groups, PACK))
    side.finish()


def run_turn(side, experts, h, back, rows, before, after):
    features, tokens = h.shape
    merge, send = before is not None, after is not None
    operands, specs, scratch = [h], [VMEM], []
    shapes, outs = [jax.ShapeDtypeStruct(h.shape, h.dtype)], [VMEM]
    if merge:
        operands += [back, rows]
        specs += [VMEM, plane((8, tokens), before)]
        scratch += [pltpu.VMEM((experts, 16, LANES), jnp.float32)]
    if send:
        operands += [rows]
        specs += [plane((8, tokens), after)]
        shapes += [jax.ShapeDtypeStruct((experts * TILES, 2, LANES), jnp.bfloat16)]
        outs += [VMEM]
    return call_with_side(
        functools.partial(turn_kernel, merge, send), side, operands, specs, shapes, outs, scratch,
        name="turn",
    )


def expert_kernel(
    side, scal_ref, blocks_ref, gain_ref, router_ref, lane_ref, other_ref, out_ref,
    win_ref, wout_ref, wide_ref, sems,
):
    core = scal_ref[0]

    @pl.when(core == 0)
    def _():
        pltpu.make_async_copy(lane_ref, win_ref, sems.at[0]).start()
        pltpu.make_async_copy(other_ref, wout_ref, sems.at[1]).start()

    @pl.when(core != 0)
    def _():
        pltpu.make_async_copy(other_ref, win_ref, sems.at[0]).start()
        pltpu.make_async_copy(lane_ref, wout_ref, sems.at[1]).start()

    side.start()
    width = win_ref.shape[1]
    groups = wide_ref.shape[0]
    blocks = load_blocks(blocks_ref, wide_ref)
    parts = [group[:, None] for group in unpack(blocks, 0)[0:3]]
    tall = jnp.concatenate(parts, axis=1).reshape(width, LANES)
    wide = tall.T[0:PACK]
    mean_square = jnp.mean(wide * wide, axis=1, keepdims=True)
    normed = (wide * lax.rsqrt(mean_square + 1e-06) * gain_ref[...]).astype(jnp.bfloat16)
    logit = jnp.sum(normed.astype(jnp.float32) * router_ref[...], axis=1, keepdims=True)
    gate = jax.nn.sigmoid(logit).astype(jnp.bfloat16).astype(jnp.float32)
    pltpu.make_async_copy(lane_ref, win_ref, sems.at[0]).wait()
    pre_act = lax.dot_general(
        normed, win_ref[...], (((1,), (1,)), ((), ())), preferred_element_type=jnp.float32
    )
    side.forward()
    active = jax.nn.gelu(pre_act, approximate=True).astype(jnp.bfloat16)
    pltpu.make_async_copy(lane_ref, wout_ref, sems.at[1]).wait()
    output = jnp.dot(active, wout_ref[...], preferred_element_type=jnp.float32)
    weighted = output * gate
    spread = jnp.broadcast_to(gate, (PACK, LANES))
    zeros = jnp.zeros_like(weighted)
    tall = jnp.concatenate([weighted, zeros], axis=0).T.reshape(groups, 3, 8, LANES)
    gates = jnp.concatenate([spread, jnp.zeros_like(spread)], axis=0).T[0:8]
    gates = jnp.broadcast_to(gates[None], (groups, 8, LANES))
    packed = pack(tall[:, 0], tall[:, 1], tall[:, 2], 0, gates)
    for number in range(groups):
        store_block(out_ref, number, packed[number])
    side.finish()


def run_expert(side, layer, scal, blocks, gains, routers, lane_w, other_w):
    hidden, width = lane_w.shape
    return call_with_side(
        expert_kernel,
        side,
        [scal, blocks, gains, routers, lane_w, other_w],
        [SMEM, VMEM, plane((1, width), layer), plane((1, width), layer), HBM, HBM],
        [jax.ShapeDtypeStruct(blocks.shape, jnp.bfloat16)],
        [VMEM],
        [
            pltpu.VMEM((hidden, width), jnp.bfloat16),
            pltpu.VMEM((hidden, width), jnp.bfloat16),
            pltpu.VMEM((blocks.shape[0] // TILES, 16, LANES), jnp.float32),
            pltpu.SemaphoreType.DMA((2,)),
        ],
        cost_estimate=pl.CostEstimate(
            flops=4 * PACK * hidden * width, bytes_accessed=4 * hidden * width, transcendentals=0
        ),
        name="expert",
    )


def plane(shape, *lead):
    return pl.BlockSpec((None,) * len(lead) + shape, lambda i: lead + (0,) * len(shape))


def place_tokens(routes, experts):
    tokens = routes.shape[1]
    ids = jnp.arange(experts, dtype=jnp.int32)
    first = routes[:, :, 0:1] == ids
    second = routes[:, :, 1:2] == ids
    named = (first | second).astype(jnp.bfloat16)
    earlier = jnp.tril(jnp.ones((tokens, tokens), jnp.bfloat16), -1)
    rank = jnp.einsum("ut,lte->lue", earlier, named, preferred_element_type=jnp.float32)
    rank = rank.astype(jnp.int32) + ids * PACK
    slot_first = jnp.sum(jnp.where(first, rank, 0), axis=2)
    slot_second = jnp.sum(jnp.where(second, rank, 0), axis=2)
    blank = jnp.zeros_like(slot_first)
    return jnp.stack([slot_first, slot_second] + [blank] * 6, axis=1)


def join(*values):
    return lax.optimization_barrier(values)


def local(inputs, routes, norm_gains, routers, expert_in, expert_out):
    sections = lax.axis_size("section")
    experts = lax.axis_size("expert")
    section_pos = lax.axis_index("section")
    repeats, _, _, hidden, width = expert_in.shape
    layers = repeats * sections
    steps, held = ring_plan(sections, layers, PARTS, LEAD)
    size = hidden // PARTS
    scal = jnp.stack([section_pos % 2, section_pos]).astype(jnp.int32)

    buffers = {("in", r): (expert_in, (r, 0, 0)) for r in range(repeats)}
    buffers.update({("out", r): (expert_out, (r, 0, 0)) for r in range(repeats)})
    every = [(lane, y) for lane in range(2) for y in range(sections // 2)]
    table, wanted = [], []

    def source_of(lane, y, i):
        q, part = i // PARTS, i % PARTS
        if q % sections // 2 != y:
            _, number, place = held[lane][y][i]
            return ("ring", number), place * size
        name = ("in", "out")[lane] if q % 2 == lane else "swapped"
        return (name, q // sections), part * size

    def add_pick(by_section):
        choices = sorted(set(by_section.values()))
        table.append([choices.index(by_section.get(s, choices[0])) for s in range(sections)])
        wanted.append(choices)
        return len(table) - 1

    swap_rows = [
        [
            add_pick({2 * y + lane: ((("out", "in")[lane], r), part * size) for lane, y in every})
            for part in range(PARTS)
        ]
        for r in range(repeats)
    ]
    ring_rows = [
        [
            add_pick({2 * y + lane: source_of(lane, y, i) for lane, y, _, i, at in moves if at == place})
            for place in sorted({move[4] for move in moves})
        ]
        for moves in steps
    ]
    layer_rows = [
        [
            add_pick({2 * y + lane: source_of(lane, y, q * PARTS + part) for lane, y in every})
            for part in range(PARTS)
        ]
        for q in range(layers)
    ]
    tab = jnp.asarray(np.array(table, np.int32).T)[section_pos]

    def side_of(tab, *jobs):
        names = sorted({name for rows in jobs for row in rows for name, _ in wanted[row]})
        found = [buffers[name] for name in names]
        plans = [
            tuple(
                (row, tuple((names.index(name), start) for name, start in wanted[row]))
                for row in rows
            )
            for rows in jobs
        ]
        return tab, plans, [array for array, _ in found], [at for _, at in found], size, width

    def picked(rows, tab):
        return pick(side_of(tab, rows))

    def swapped(value):
        return lax.ppermute(value, "section", [(s, s ^ 1) for s in range(sections)])

    def ring(number, value):
        moves = steps[number - 1]
        pairs = sorted({(2 * y + lane, 2 * target + lane) for lane, y, target, _, _ in moves})
        return lax.ppermute(value, "section", pairs)

    def arrival(q):
        parts = range(q * PARTS, (q + 1) * PARTS)
        return max(stock[i][0] for lane in held for stock in lane for i in parts)

    mine = lax.all_to_all(routes[:, 0], "section", split_axis=1, concat_axis=0, tiled=False)
    mine = jnp.transpose(mine, (1, 0, 2, 3)).reshape(layers, -1, 2)
    rows = place_tokens(mine, experts)
    small = jnp.stack([norm_gains[:, 0], routers[:, 0, 0]])
    small = jnp.broadcast_to(small[None], (sections,) + small.shape)
    small = lax.all_to_all(small, "section", split_axis=0, concat_axis=0, tiled=True)
    small = jnp.transpose(small, (1, 2, 0, 3)).reshape(2, layers, 1, width).astype(jnp.float32)
    gains, gate_rows = small[0], small[1]
    h = jnp.transpose(inputs[0], (1, 0))

    buffers[("swapped", 0)] = (swapped(picked(swap_rows[0], tab)), ())
    later = swapped(picked(swap_rows[1], tab))
    flying = None
    for number in range(1, LEAD + 1):
        started = ring(number, picked(ring_rows[number - 1], tab))
        if number == LEAD:
            h, tab = join(h, tab)
            h, blocks = run_turn(side_of(tab), experts, h, None, rows, None, 0)
            blocks, tab = join(send_blocks(blocks), tab)
        if flying is not None:
            flying, tab = join(flying, tab)
            buffers[("ring", number - 1)] = (flying, ())
        if number == 2:
            later, tab, rows, gains, gate_rows, h = join(later, tab, rows, gains, gate_rows, h)
            buffers[("swapped", 1)] = (later, ())
        flying = started
    flying, tab, blocks = join(flying, tab, blocks)
    buffers[("ring", LEAD)] = (flying, ())
    lane_w = picked(layer_rows[0], tab)
    coming = (lane_w, swapped(lane_w))
    flying = ring(LEAD + 1, picked(ring_rows[LEAD], tab))
    blocks, tab, *coming = join(blocks, tab, *coming)

    for q in range(layers):
        number = LEAD + 1 + q
        if q:
            jobs = ([ring_rows[number - 1]] if number <= len(steps) else []) + (
                [] if coming else [layer_rows[q]]
            )
            h, blocks, *extra = run_turn(side_of(tab, *jobs), experts, h, back, rows, q - 1, q)
            flying = ring(number, extra.pop(0)) if number <= len(steps) else None
            if not coming:
                coming = (extra[0], swapped(extra[0]))
            blocks, tab, *coming = join(send_blocks(blocks), tab, *coming)
        jobs = [layer_rows[q + 1]] if q + 1 < layers and arrival(q + 1) < number else []
        back, *extra = run_expert(
            side_of(tab, *jobs), q, scal, blocks, gains, gate_rows, *coming
        )
        coming = (extra[0], swapped(extra[0])) if jobs else None
        if flying is None:
            back, tab = join(send_blocks(back), tab)
        else:
            back, tab, flying = join(send_blocks(back), tab, flying)
            buffers[("ring", number)] = (flying, ())

    (h,) = run_turn(side_of(tab), experts, h, back, rows, layers - 1, None)
    return jnp.transpose(h, (1, 0))[None]


def solution(mesh):
    return jax.shard_map(
        local,
        mesh=mesh,
        in_specs=(
            P("section", None, "expert"),
            P(None, "section", None, None, None),
            P(None, "section", None),
            P(None, "section", "expert", None),
            P(None, "section", "expert", None, None),
            P(None, "section", "expert", None, None),
        ),
        out_specs=P("section", None, "expert"),
        check_vma=False,
    )
```

```python
import functools

import jax
import jax.numpy as jnp
import numpy as np
from jax import lax
from jax.experimental import pallas as pl
from jax.experimental.pallas import tpu as pltpu
from jax.sharding import PartitionSpec as P

VMEM_LIMIT = 64400 * 1024
HBM = pl.BlockSpec(memory_space=pltpu.HBM)
SMEM = pl.BlockSpec(memory_space=pltpu.SMEM)
VMEM = pl.BlockSpec(memory_space=pltpu.VMEM)
DIRS = (1, -1)


PACK = 64
SLOTS = 48
FAST = 8
ROWS = 10
PARTS = 2
LEAD = 6


def ring_plan(sections, layers, parts, lead):
    chips = sections // 2
    items = layers * parts
    held = [
        [
            {i: (0, 0, 0) for i in range(items) if (i // parts) % sections // 2 == y}
            for y in range(chips)
        ]
        for _ in DIRS
    ]
    steps = []
    while any(len(stock) < items for lane in held for stock in lane):
        number = len(steps) + 1
        moves = []
        for lane, step in enumerate(DIRS):
            for y in range(chips):
                target = (y + step) % chips
                there = held[lane][target]
                options = sorted(i for i, at in held[lane][y].items() if at[0] < number and i not in there)
                for place, i in enumerate(options[: 1 if number <= lead else parts]):
                    moves.append((lane, y, target, i, place))
        steps.append(moves)
        for lane, _, target, i, place in moves:
            held[lane][target][i] = (number + (number < lead), number, place)
    return steps, held


class Reads:
    def __init__(self, rows, places, size, tab_ref, sources, hold_ref, sems):
        self.rows, self.places, self.size = rows, places, size
        self.tab_ref, self.sources = tab_ref, sources
        self.hold_ref, self.sems = hold_ref, sems

    def part_of(self, ref, part):
        return ref.at[pl.ds(pl.multiple_of(part * self.size, self.size), self.size)]

    def copy(self, part, choice):
        number, start = choice
        view = self.sources[number].at[self.places[number] + (pl.ds(start, self.size),)]
        return pltpu.make_async_copy(view, self.part_of(self.hold_ref, part), self.sems.at[part])

    def start(self):
        for part, (row, choices) in enumerate(self.rows):
            wish = self.tab_ref[row]
            for number, choice in enumerate(choices):

                @pl.when(wish == number)
                def _(part=part, choice=choice):
                    self.copy(part, choice).start()

    def wait(self, part):
        to = self.part_of(self.hold_ref, part)
        pltpu.make_async_copy(to, to, self.sems.at[part]).wait()

    def forward(self, out_ref, sems):
        for part in range(len(self.rows)):
            self.wait(part)
            self.leave(part, out_ref, sems).start()

    def finish(self, out_ref, sems):
        for part in range(len(self.rows)):
            self.leave(part, out_ref, sems).wait()

    def leave(self, part, out_ref, sems):
        return pltpu.make_async_copy(
            self.part_of(self.hold_ref, part), self.part_of(out_ref, part), sems.at[part]
        )


class Side:
    def __init__(self, side):
        self.tab, self.jobs, arrays, self.places, self.size, width = side
        self.operands = [self.tab] + arrays
        self.in_specs = [SMEM] + [HBM] * len(arrays)
        shapes = [(self.size * len(rows), width) for rows in self.jobs]
        self.out_shapes = [jax.ShapeDtypeStruct(shape, jnp.bfloat16) for shape in shapes]
        self.out_specs = [HBM] * len(self.jobs)
        self.scratch = []
        for rows, shape in zip(self.jobs, shapes):
            self.scratch += [pltpu.VMEM(shape, jnp.bfloat16)]
            self.scratch += [pltpu.SemaphoreType.DMA((len(rows),))] * 2

    def bind(self, inputs, outputs, scratch):
        self.outputs = outputs
        self.reads = [
            Reads(rows, self.places, self.size, inputs[0], inputs[1:], hold_ref, in_sems)
            for rows, hold_ref, in_sems in zip(self.jobs, scratch[0::3], scratch[1::3])
        ]
        self.out_sems = scratch[2::3]

    def start(self):
        for reads in self.reads:
            reads.start()

    def forward(self):
        for reads, out_ref, sems in zip(self.reads, self.outputs, self.out_sems):
            reads.forward(out_ref, sems)

    def finish(self):
        for reads, out_ref, sems in zip(self.reads, self.outputs, self.out_sems):
            reads.finish(out_ref, sems)


def call_with_side(kernel, side, operands, in_specs, shapes, out_specs, scratch, **options):
    beside = Side(side)
    counts = [len(operands), len(beside.operands), len(shapes), len(beside.out_shapes), len(scratch)]

    def body(*refs):
        cuts = np.cumsum(counts)
        groups = [refs[end - count : end] for count, end in zip(counts, cuts)]
        beside.bind(groups[1], groups[3], refs[cuts[-1] :])
        kernel(beside, *groups[0], *groups[2], *groups[4])

    return pl.pallas_call(
        body,
        out_shape=tuple(shapes) + tuple(beside.out_shapes),
        grid=(1,),
        in_specs=list(in_specs) + beside.in_specs,
        out_specs=tuple(out_specs) + tuple(beside.out_specs),
        scratch_shapes=list(scratch) + beside.scratch,
        compiler_params=pltpu.CompilerParams(vmem_limit_bytes=VMEM_LIMIT),
        **options,
    )(*operands, *beside.operands)


def copy_kernel(side):
    side.start()
    side.forward()
    side.finish()


def pick(side):
    return call_with_side(copy_kernel, side, [], [], [], [], [], name="pick")[0]


LANES = 128


def turned(value, lanes):
    return pltpu.roll(value, lanes % LANES, value.ndim - 1)


def lanes_of(value):
    return lax.broadcasted_iota(jnp.int32, (1,) * (value.ndim - 1) + (LANES,), value.ndim - 1)


def fold_tail(third, at):
    axis = third.ndim - 1
    spread = pltpu.roll(turned(third, -at - 32), 0, axis, stride=16, stride_axis=axis - 1)
    place = lax.broadcasted_iota(jnp.int32, third.shape, axis) // 16
    own = place == lax.broadcasted_iota(jnp.int32, third.shape, axis - 1)
    return jnp.sum(jnp.where(own, spread, 0.0), axis=axis - 1, keepdims=True)


def unfold_tail(row, at):
    value = jnp.broadcast_to(turned(row, at + 32), row.shape[:-2] + (8, LANES))
    number = lax.broadcasted_iota(jnp.int32, value.shape, value.ndim - 2)
    for step in (1, 2, 4):
        value = jnp.where((number & step) != 0, turned(value, -16 * step), value)
    return value


def pack(first, second, third, at, gates=None):
    lanes = lanes_of(first)
    top = jnp.where(
        lanes < SLOTS,
        turned(first, -at),
        jnp.where(lanes < 2 * SLOTS, turned(second, SLOTS - at), turned(third, 2 * SLOTS - at)),
    )
    tail = fold_tail(third, at)
    axis = first.ndim - 2
    number = lax.broadcasted_iota(jnp.int32, top.shape, axis)
    last = jnp.broadcast_to(tail, top.shape)
    if gates is not None:
        last = jnp.where(number == 0, last, gates)
    return jnp.concatenate([top, last], axis=axis)


def unpack(blocks, at):
    top, last = blocks[..., 0:8, :], blocks[..., 8:16, :]
    lanes = lanes_of(blocks)
    third = jnp.where(
        lanes - at < 32, turned(top, at - 2 * SLOTS), unfold_tail(last[..., 0:1, :], at)
    )
    return turned(top, at), turned(top, at - SLOTS), third, turned(last, at)


def unpack_pairs(back):
    pairs = back.shape[0] // 2
    split = back.reshape(pairs, 2, 16, LANES)
    low = lanes_of(back) < PACK
    both = zip(unpack(split[:, 0], 0), unpack(split[:, 1], PACK))
    groups = [jnp.where(low, even, odd) for even, odd in both]
    gates = jnp.broadcast_to(groups[3][:, 1:2], groups[0].shape)
    return jnp.concatenate(groups[0:3] + [gates], axis=1)


TILES = ROWS // 2


def load_blocks(ref, wide_ref):
    for number in range(wide_ref.shape[0]):
        block = ref[TILES * number : TILES * (number + 1)].reshape(ROWS, LANES)
        wide_ref[number, 0:ROWS] = block.astype(jnp.float32)
    return wide_ref[...]


def store_block(ref, number, block):
    rows = block.astype(jnp.bfloat16).reshape(8, 2, LANES)
    ref[TILES * number : TILES * (number + 1)] = rows[0:TILES]


def place_of(expert, experts):
    return expert % FAST * (experts // FAST) + expert // FAST


def send_blocks(value):
    experts = lax.axis_size("expert")
    slow = experts // FAST
    along_z = [[x * FAST + z for z in range(FAST)] for x in range(slow)]
    along_x = [[x * FAST + z for x in range(slow)] for z in range(FAST)]

    def exchange(some, groups):
        return lax.all_to_all(
            some, "expert", split_axis=0, concat_axis=0, axis_index_groups=groups, tiled=True
        )

    half = exchange(value, along_z).reshape(FAST, slow, TILES, 2, LANES)
    half = jnp.transpose(half, (1, 0, 2, 3, 4)).reshape(value.shape)
    return exchange(half, along_x)


def turn_kernel(merge, send, side, *refs):
    side.start()
    refs = list(refs)
    h_ref = refs.pop(0)
    if merge:
        back_ref, row_ref = refs.pop(0), refs.pop(0)
    if send:
        next_ref = refs.pop(0)
    hnew_ref = refs.pop(0)
    features, tokens = h_ref.shape
    held = h_ref[...]
    if merge:
        tiles = unpack_pairs(load_blocks(back_ref, refs.pop())).astype(jnp.bfloat16)
        offset = lax.broadcasted_iota(jnp.int32, (4 * PACK, tokens), 0)
        first, second = row_ref[0:1, :] - offset, row_ref[1:2, :] - offset
        update = jnp.zeros((32, tokens), jnp.float32)
        for turn in range(tiles.shape[0] // 2):
            base = turn * 4 * PACK
            onehot = jnp.where((first == base) | (second == base), 1.0, 0.0)
            pair = jnp.concatenate([tiles[2 * turn], tiles[2 * turn + 1]], axis=1)
            update += jnp.dot(
                pair, onehot.astype(jnp.bfloat16), preferred_element_type=jnp.float32
            )
        change = update[0:features] * (1.0 / update[features:features + 1])
        held = (held.astype(jnp.float32) + change).astype(jnp.bfloat16)
    hnew_ref[...] = held
    side.forward()
    if send:
        out_ref = refs.pop(0)
        offset = lax.broadcasted_iota(jnp.int32, (tokens, 4 * PACK), 1)
        col = next_ref[...].astype(jnp.float32).T.astype(jnp.int32)
        first, second = col[:, 0:1] - offset, col[:, 1:2] - offset
        experts = out_ref.shape[0] // TILES
        for turn in range(experts // 4):
            base = turn * 4 * PACK
            onehot = jnp.where((first == base) | (second == base), 1.0, 0.0)
            found = jnp.dot(held, onehot.astype(jnp.bfloat16), preferred_element_type=jnp.float32)
            for half in range(2):
                tile = found[:, LANES * half : LANES * (half + 1)]
                groups = tile[0:8], tile[8:16], tile[16:24]
                number = turn * 4 + half * 2
                places = [place_of(e, experts) for e in (number, number + 1)]
                store_block(out_ref, places[0], pack(*groups, 0))
                store_block(out_ref, places[1], pack(*groups, PACK))
    side.finish()


def run_turn(side, experts, h, back, rows, before, after):
    features, tokens = h.shape
    merge, send = before is not None, after is not None
    operands, specs, scratch = [h], [VMEM], []
    shapes, outs = [jax.ShapeDtypeStruct(h.shape, h.dtype)], [VMEM]
    if merge:
        operands += [back, rows]
        specs += [VMEM, plane((8, tokens), before)]
        scratch += [pltpu.VMEM((experts, 16, LANES), jnp.float32)]
    if send:
        operands += [rows]
        specs += [plane((8, tokens), after)]
        shapes += [jax.ShapeDtypeStruct((experts * TILES, 2, LANES), jnp.bfloat16)]
        outs += [VMEM]
    return call_with_side(
        functools.partial(turn_kernel, merge, send), side, operands, specs, shapes, outs, scratch,
        name="turn",
    )


def expert_kernel(
    side, scal_ref, blocks_ref, gain_ref, router_ref, lane_ref, other_ref, out_ref,
    win_ref, wout_ref, wide_ref, sems,
):
    core = scal_ref[0]

    @pl.when(core == 0)
    def _():
        pltpu.make_async_copy(lane_ref, win_ref, sems.at[0]).start()
        pltpu.make_async_copy(other_ref, wout_ref, sems.at[1]).start()

    @pl.when(core != 0)
    def _():
        pltpu.make_async_copy(other_ref, win_ref, sems.at[0]).start()
        pltpu.make_async_copy(lane_ref, wout_ref, sems.at[1]).start()

    side.start()
    width = win_ref.shape[1]
    groups = wide_ref.shape[0]
    blocks = load_blocks(blocks_ref, wide_ref)
    parts = [group[:, None] for group in unpack(blocks, 0)[0:3]]
    tall = jnp.concatenate(parts, axis=1).reshape(width, LANES)
    wide = tall.T[0:PACK]
    mean_square = jnp.mean(wide * wide, axis=1, keepdims=True)
    normed = (wide * lax.rsqrt(mean_square + 1e-06) * gain_ref[...]).astype(jnp.bfloat16)
    logit = jnp.sum(normed.astype(jnp.float32) * router_ref[...], axis=1, keepdims=True)
    gate = jax.nn.sigmoid(logit).astype(jnp.bfloat16).astype(jnp.float32)
    pltpu.make_async_copy(lane_ref, win_ref, sems.at[0]).wait()
    pre_act = lax.dot_general(
        normed, win_ref[...], (((1,), (1,)), ((), ())), preferred_element_type=jnp.float32
    )
    side.forward()
    active = jax.nn.gelu(pre_act, approximate=True).astype(jnp.bfloat16)
    pltpu.make_async_copy(lane_ref, wout_ref, sems.at[1]).wait()
    output = jnp.dot(active, wout_ref[...], preferred_element_type=jnp.float32)
    weighted = output * gate
    spread = jnp.broadcast_to(gate, (PACK, LANES))
    zeros = jnp.zeros_like(weighted)
    tall = jnp.concatenate([weighted, zeros], axis=0).T.reshape(groups, 3, 8, LANES)
    gates = jnp.concatenate([spread, jnp.zeros_like(spread)], axis=0).T[0:8]
    gates = jnp.broadcast_to(gates[None], (groups, 8, LANES))
    packed = pack(tall[:, 0], tall[:, 1], tall[:, 2], 0, gates)
    for number in range(groups):
        store_block(out_ref, place_of(number, groups), packed[number])
    side.finish()


def run_expert(side, layer, scal, blocks, gains, routers, lane_w, other_w):
    hidden, width = lane_w.shape
    return call_with_side(
        expert_kernel,
        side,
        [scal, blocks, gains, routers, lane_w, other_w],
        [SMEM, VMEM, plane((1, width), layer), plane((1, width), layer), HBM, HBM],
        [jax.ShapeDtypeStruct(blocks.shape, jnp.bfloat16)],
        [VMEM],
        [
            pltpu.VMEM((hidden, width), jnp.bfloat16),
            pltpu.VMEM((hidden, width), jnp.bfloat16),
            pltpu.VMEM((blocks.shape[0] // TILES, 16, LANES), jnp.float32),
            pltpu.SemaphoreType.DMA((2,)),
        ],
        cost_estimate=pl.CostEstimate(
            flops=4 * PACK * hidden * width, bytes_accessed=4 * hidden * width, transcendentals=0
        ),
        name="expert",
    )


def plane(shape, *lead):
    return pl.BlockSpec((None,) * len(lead) + shape, lambda i: lead + (0,) * len(shape))


def place_tokens(routes, experts):
    tokens = routes.shape[1]
    ids = jnp.arange(experts, dtype=jnp.int32)
    first = routes[:, :, 0:1] == ids
    second = routes[:, :, 1:2] == ids
    named = (first | second).astype(jnp.bfloat16)
    earlier = jnp.tril(jnp.ones((tokens, tokens), jnp.bfloat16), -1)
    rank = jnp.einsum("ut,lte->lue", earlier, named, preferred_element_type=jnp.float32)
    rank = rank.astype(jnp.int32) + ids * PACK
    slot_first = jnp.sum(jnp.where(first, rank, 0), axis=2)
    slot_second = jnp.sum(jnp.where(second, rank, 0), axis=2)
    blank = jnp.zeros_like(slot_first)
    return jnp.stack([slot_first, slot_second] + [blank] * 6, axis=1)


def join(*values):
    return lax.optimization_barrier(values)


def local(inputs, routes, norm_gains, routers, expert_in, expert_out):
    sections = lax.axis_size("section")
    experts = lax.axis_size("expert")
    section_pos = lax.axis_index("section")
    repeats, _, _, hidden, width = expert_in.shape
    layers = repeats * sections
    steps, held = ring_plan(sections, layers, PARTS, LEAD)
    size = hidden // PARTS
    scal = jnp.stack([section_pos % 2, section_pos]).astype(jnp.int32)

    buffers = {("in", r): (expert_in, (r, 0, 0)) for r in range(repeats)}
    buffers.update({("out", r): (expert_out, (r, 0, 0)) for r in range(repeats)})
    every = [(lane, y) for lane in range(2) for y in range(sections // 2)]
    table, wanted = [], []

    def source_of(lane, y, i):
        q, part = i // PARTS, i % PARTS
        if q % sections // 2 != y:
            _, number, place = held[lane][y][i]
            return ("ring", number), place * size
        name = ("in", "out")[lane] if q % 2 == lane else "swapped"
        return (name, q // sections), part * size

    def add_pick(by_section):
        choices = sorted(set(by_section.values()))
        table.append([choices.index(by_section.get(s, choices[0])) for s in range(sections)])
        wanted.append(choices)
        return len(table) - 1

    swap_rows = [
        [
            add_pick({2 * y + lane: ((("out", "in")[lane], r), part * size) for lane, y in every})
            for part in range(PARTS)
        ]
        for r in range(repeats)
    ]
    ring_rows = [
        [
            add_pick({2 * y + lane: source_of(lane, y, i) for lane, y, _, i, at in moves if at == place})
            for place in sorted({move[4] for move in moves})
        ]
        for moves in steps
    ]
    layer_rows = [
        [
            add_pick({2 * y + lane: source_of(lane, y, q * PARTS + part) for lane, y in every})
            for part in range(PARTS)
        ]
        for q in range(layers)
    ]
    tab = jnp.asarray(np.array(table, np.int32).T)[section_pos]

    def side_of(tab, *jobs):
        names = sorted({name for rows in jobs for row in rows for name, _ in wanted[row]})
        found = [buffers[name] for name in names]
        plans = [
            tuple(
                (row, tuple((names.index(name), start) for name, start in wanted[row]))
                for row in rows
            )
            for rows in jobs
        ]
        return tab, plans, [array for array, _ in found], [at for _, at in found], size, width

    def picked(rows, tab):
        return pick(side_of(tab, rows))

    def swapped(value):
        return lax.ppermute(value, "section", [(s, s ^ 1) for s in range(sections)])

    def ring(number, value):
        moves = steps[number - 1]
        pairs = sorted({(2 * y + lane, 2 * target + lane) for lane, y, target, _, _ in moves})
        return lax.ppermute(value, "section", pairs)

    def arrival(q):
        parts = range(q * PARTS, (q + 1) * PARTS)
        return max(stock[i][0] for lane in held for stock in lane for i in parts)

    mine = lax.all_to_all(routes[:, 0], "section", split_axis=1, concat_axis=0, tiled=False)
    small = jnp.stack([norm_gains[:, 0], routers[:, 0, 0]])
    small = jnp.broadcast_to(small[None], (sections,) + small.shape)
    small = lax.all_to_all(small, "section", split_axis=0, concat_axis=0, tiled=True)
    h = jnp.transpose(inputs[0], (1, 0))

    mine_first = swapped(picked(swap_rows[0], tab))
    mine_first, tab, mine, small = join(mine_first, tab, mine, small)
    buffers[("swapped", 0)] = (mine_first, ())
    later = swapped(picked(swap_rows[1], tab))
    mine = jnp.transpose(mine, (1, 0, 2, 3)).reshape(layers, -1, 2)
    rows = place_tokens(mine, experts)
    small = jnp.transpose(small, (1, 2, 0, 3)).reshape(2, layers, 1, width).astype(jnp.float32)
    gains, gate_rows = small[0], small[1]
    flying = None
    for number in range(1, LEAD + 1):
        started = ring(number, picked(ring_rows[number - 1], tab))
        if number == LEAD:
            h, tab = join(h, tab)
            h, blocks = run_turn(side_of(tab), experts, h, None, rows, None, 0)
            blocks, tab = join(send_blocks(blocks), tab)
        if flying is not None:
            flying, tab = join(flying, tab)
            buffers[("ring", number - 1)] = (flying, ())
        if number == 2:
            later, tab, rows, gains, gate_rows, h = join(later, tab, rows, gains, gate_rows, h)
            buffers[("swapped", 1)] = (later, ())
        flying = started
    flying, tab, blocks = join(flying, tab, blocks)
    buffers[("ring", LEAD)] = (flying, ())
    lane_w = picked(layer_rows[0], tab)
    coming = (lane_w, swapped(lane_w))
    flying = ring(LEAD + 1, picked(ring_rows[LEAD], tab))
    blocks, tab, *coming = join(blocks, tab, *coming)

    for q in range(layers):
        number = LEAD + 1 + q
        if q:
            jobs = ([ring_rows[number - 1]] if number <= len(steps) else []) + (
                [] if coming else [layer_rows[q]]
            )
            h, blocks, *extra = run_turn(side_of(tab, *jobs), experts, h, back, rows, q - 1, q)
            flying = ring(number, extra.pop(0)) if number <= len(steps) else None
            if not coming:
                coming = (extra[0], swapped(extra[0]))
            blocks, tab, *coming = join(send_blocks(blocks), tab, *coming)
        jobs = [layer_rows[q + 1]] if q + 1 < layers and arrival(q + 1) < number else []
        back, *extra = run_expert(
            side_of(tab, *jobs), q, scal, blocks, gains, gate_rows, *coming
        )
        coming = (extra[0], swapped(extra[0])) if jobs else None
        if flying is None:
            back, tab = join(send_blocks(back), tab)
        else:
            back, tab, flying = join(send_blocks(back), tab, flying)
            buffers[("ring", number)] = (flying, ())

    (h,) = run_turn(side_of(tab), experts, h, back, rows, layers - 1, None)
    return jnp.transpose(h, (1, 0))[None]


def solution(mesh):
    return jax.shard_map(
        local,
        mesh=mesh,
        in_specs=(
            P("section", None, "expert"),
            P(None, "section", None, None, None),
            P(None, "section", None),
            P(None, "section", "expert", None),
            P(None, "section", "expert", None, None),
            P(None, "section", "expert", None, None),
        ),
        out_specs=P("section", None, "expert"),
        check_vma=False,
    )
```

```python
import functools

import jax
import jax.numpy as jnp
import numpy as np
from jax import lax
from jax.experimental import pallas as pl
from jax.experimental.pallas import tpu as pltpu
from jax.sharding import PartitionSpec as P

VMEM_LIMIT = 64400 * 1024
HBM = pl.BlockSpec(memory_space=pltpu.HBM)
SMEM = pl.BlockSpec(memory_space=pltpu.SMEM)
VMEM = pl.BlockSpec(memory_space=pltpu.VMEM)
DIRS = (1, -1)


PACK = 64
SLOTS = 48
ROWS = 10
PARTS = 2
LEAD = 6


def ring_plan(sections, layers, parts, lead):
    chips = sections // 2
    items = layers * parts
    held = [
        [
            {i: (0, 0, 0) for i in range(items) if (i // parts) % sections // 2 == y}
            for y in range(chips)
        ]
        for _ in DIRS
    ]
    steps = []
    while any(len(stock) < items for lane in held for stock in lane):
        number = len(steps) + 1
        moves = []
        for lane, step in enumerate(DIRS):
            for y in range(chips):
                target = (y + step) % chips
                there = held[lane][target]
                options = sorted(i for i, at in held[lane][y].items() if at[0] < number and i not in there)
                for place, i in enumerate(options[: 1 if number <= lead else parts]):
                    moves.append((lane, y, target, i, place))
        steps.append(moves)
        for lane, _, target, i, place in moves:
            held[lane][target][i] = (number + (number < lead), number, place)
    return steps, held


class Reads:
    def __init__(self, rows, places, size, tab_ref, sources, hold_ref, sems):
        self.rows, self.places, self.size = rows, places, size
        self.tab_ref, self.sources = tab_ref, sources
        self.hold_ref, self.sems = hold_ref, sems

    def part_of(self, ref, part):
        return ref.at[pl.ds(pl.multiple_of(part * self.size, self.size), self.size)]

    def copy(self, part, choice):
        number, start = choice
        view = self.sources[number].at[self.places[number] + (pl.ds(start, self.size),)]
        return pltpu.make_async_copy(view, self.part_of(self.hold_ref, part), self.sems.at[part])

    def start(self):
        for part, (row, choices) in enumerate(self.rows):
            wish = self.tab_ref[row]
            for number, choice in enumerate(choices):

                @pl.when(wish == number)
                def _(part=part, choice=choice):
                    self.copy(part, choice).start()

    def wait(self, part):
        to = self.part_of(self.hold_ref, part)
        pltpu.make_async_copy(to, to, self.sems.at[part]).wait()

    def forward(self, out_ref, sems):
        for part in range(len(self.rows)):
            self.wait(part)
            self.leave(part, out_ref, sems).start()

    def finish(self, out_ref, sems):
        for part in range(len(self.rows)):
            self.leave(part, out_ref, sems).wait()

    def leave(self, part, out_ref, sems):
        return pltpu.make_async_copy(
            self.part_of(self.hold_ref, part), self.part_of(out_ref, part), sems.at[part]
        )


class Side:
    def __init__(self, side):
        self.tab, self.jobs, arrays, self.places, self.size, width = side
        self.operands = [self.tab] + arrays
        self.in_specs = [SMEM] + [HBM] * len(arrays)
        shapes = [(self.size * len(rows), width) for rows in self.jobs]
        self.out_shapes = [jax.ShapeDtypeStruct(shape, jnp.bfloat16) for shape in shapes]
        self.out_specs = [HBM] * len(self.jobs)
        self.scratch = []
        for rows, shape in zip(self.jobs, shapes):
            self.scratch += [pltpu.VMEM(shape, jnp.bfloat16)]
            self.scratch += [pltpu.SemaphoreType.DMA((len(rows),))] * 2

    def bind(self, inputs, outputs, scratch):
        self.outputs = outputs
        self.reads = [
            Reads(rows, self.places, self.size, inputs[0], inputs[1:], hold_ref, in_sems)
            for rows, hold_ref, in_sems in zip(self.jobs, scratch[0::3], scratch[1::3])
        ]
        self.out_sems = scratch[2::3]

    def start(self):
        for reads in self.reads:
            reads.start()

    def forward(self):
        for reads, out_ref, sems in zip(self.reads, self.outputs, self.out_sems):
            reads.forward(out_ref, sems)

    def finish(self):
        for reads, out_ref, sems in zip(self.reads, self.outputs, self.out_sems):
            reads.finish(out_ref, sems)


def call_with_side(kernel, side, operands, in_specs, shapes, out_specs, scratch, **options):
    beside = Side(side)
    counts = [len(operands), len(beside.operands), len(shapes), len(beside.out_shapes), len(scratch)]

    def body(*refs):
        cuts = np.cumsum(counts)
        groups = [refs[end - count : end] for count, end in zip(counts, cuts)]
        beside.bind(groups[1], groups[3], refs[cuts[-1] :])
        kernel(beside, *groups[0], *groups[2], *groups[4])

    return pl.pallas_call(
        body,
        out_shape=tuple(shapes) + tuple(beside.out_shapes),
        grid=(1,),
        in_specs=list(in_specs) + beside.in_specs,
        out_specs=tuple(out_specs) + tuple(beside.out_specs),
        scratch_shapes=list(scratch) + beside.scratch,
        compiler_params=pltpu.CompilerParams(vmem_limit_bytes=VMEM_LIMIT),
        **options,
    )(*operands, *beside.operands)


def copy_kernel(side):
    side.start()
    side.forward()
    side.finish()


def pick(side):
    return call_with_side(copy_kernel, side, [], [], [], [], [], name="pick")[0]


LANES = 128


def turned(value, lanes):
    return pltpu.roll(value, lanes % LANES, value.ndim - 1)


def lanes_of(value):
    return lax.broadcasted_iota(jnp.int32, (1,) * (value.ndim - 1) + (LANES,), value.ndim - 1)


def fold_tail(third, at):
    axis = third.ndim - 1
    spread = pltpu.roll(turned(third, -at - 32), 0, axis, stride=16, stride_axis=axis - 1)
    place = lax.broadcasted_iota(jnp.int32, third.shape, axis) // 16
    own = place == lax.broadcasted_iota(jnp.int32, third.shape, axis - 1)
    return jnp.sum(jnp.where(own, spread, 0.0), axis=axis - 1, keepdims=True)


def unfold_tail(row, at):
    value = jnp.broadcast_to(turned(row, at + 32), row.shape[:-2] + (8, LANES))
    number = lax.broadcasted_iota(jnp.int32, value.shape, value.ndim - 2)
    for step in (1, 2, 4):
        value = jnp.where((number & step) != 0, turned(value, -16 * step), value)
    return value


def pack(first, second, third, at, gates=None):
    lanes = lanes_of(first)
    top = jnp.where(
        lanes < SLOTS,
        turned(first, -at),
        jnp.where(lanes < 2 * SLOTS, turned(second, SLOTS - at), turned(third, 2 * SLOTS - at)),
    )
    tail = fold_tail(third, at)
    axis = first.ndim - 2
    number = lax.broadcasted_iota(jnp.int32, top.shape, axis)
    last = jnp.broadcast_to(tail, top.shape)
    if gates is not None:
        last = jnp.where(number == 0, last, gates)
    return jnp.concatenate([top, last], axis=axis)


def unpack(blocks, at):
    top, last = blocks[..., 0:8, :], blocks[..., 8:16, :]
    lanes = lanes_of(blocks)
    third = jnp.where(
        lanes - at < 32, turned(top, at - 2 * SLOTS), unfold_tail(last[..., 0:1, :], at)
    )
    return turned(top, at), turned(top, at - SLOTS), third, turned(last, at)


def unpack_pairs(back):
    pairs = back.shape[0] // 2
    split = back.reshape(pairs, 2, 16, LANES)
    low = lanes_of(back) < PACK
    both = zip(unpack(split[:, 0], 0), unpack(split[:, 1], PACK))
    groups = [jnp.where(low, even, odd) for even, odd in both]
    gates = jnp.broadcast_to(groups[3][:, 1:2], groups[0].shape)
    return jnp.concatenate(groups[0:3] + [gates], axis=1)


TILES = ROWS // 2


def load_blocks(ref, wide_ref):
    for number in range(wide_ref.shape[0]):
        block = ref[TILES * number : TILES * (number + 1)].reshape(ROWS, LANES)
        wide_ref[number, 0:ROWS] = block.astype(jnp.float32)
    return wide_ref[...]


def store_block(ref, number, block):
    rows = block.astype(jnp.bfloat16).reshape(8, 2, LANES)
    ref[TILES * number : TILES * (number + 1)] = rows[0:TILES]


def send_blocks(value):
    return lax.all_to_all(value, "expert", split_axis=0, concat_axis=0, tiled=True)


def turn_kernel(merge, send, side, *refs):
    side.start()
    refs = list(refs)
    h_ref = refs.pop(0)
    if merge:
        back_ref, row_ref = refs.pop(0), refs.pop(0)
    if send:
        next_ref = refs.pop(0)
    hnew_ref = refs.pop(0)
    features, tokens = h_ref.shape
    held = h_ref[...]
    if merge:
        tiles = unpack_pairs(load_blocks(back_ref, refs.pop())).astype(jnp.bfloat16)
        offset = lax.broadcasted_iota(jnp.int32, (4 * PACK, tokens), 0)
        first, second = row_ref[0:1, :] - offset, row_ref[1:2, :] - offset
        update = jnp.zeros((32, tokens), jnp.float32)
        for turn in range(tiles.shape[0] // 2):
            base = turn * 4 * PACK
            onehot = jnp.where((first == base) | (second == base), 1.0, 0.0)
            pair = jnp.concatenate([tiles[2 * turn], tiles[2 * turn + 1]], axis=1)
            update += jnp.dot(
                pair, onehot.astype(jnp.bfloat16), preferred_element_type=jnp.float32
            )
        change = update[0:features] * (1.0 / update[features:features + 1])
        held = (held.astype(jnp.float32) + change).astype(jnp.bfloat16)
    hnew_ref[...] = held
    side.forward()
    if send:
        out_ref = refs.pop(0)
        offset = lax.broadcasted_iota(jnp.int32, (tokens, 4 * PACK), 1)
        col = next_ref[...].astype(jnp.float32).T.astype(jnp.int32)
        first, second = col[:, 0:1] - offset, col[:, 1:2] - offset
        for turn in range(out_ref.shape[0] // TILES // 4):
            base = turn * 4 * PACK
            onehot = jnp.where((first == base) | (second == base), 1.0, 0.0)
            found = jnp.dot(held, onehot.astype(jnp.bfloat16), preferred_element_type=jnp.float32)
            for half in range(2):
                tile = found[:, LANES * half : LANES * (half + 1)]
                groups = tile[0:8], tile[8:16], tile[16:24]
                number = turn * 4 + half * 2
                store_block(out_ref, number, pack(*groups, 0))
                store_block(out_ref, number + 1, pack(*groups, PACK))
    side.finish()


def run_turn(side, experts, h, back, rows, before, after):
    features, tokens = h.shape
    merge, send = before is not None, after is not None
    operands, specs, scratch = [h], [VMEM], []
    shapes, outs = [jax.ShapeDtypeStruct(h.shape, h.dtype)], [VMEM]
    if merge:
        operands += [back, rows]
        specs += [VMEM, plane((8, tokens), before)]
        scratch += [pltpu.VMEM((experts, 16, LANES), jnp.float32)]
    if send:
        operands += [rows]
        specs += [plane((8, tokens), after)]
        shapes += [jax.ShapeDtypeStruct((experts * TILES, 2, LANES), jnp.bfloat16)]
        outs += [VMEM]
    return call_with_side(
        functools.partial(turn_kernel, merge, send), side, operands, specs, shapes, outs, scratch,
        name="turn",
    )


def expert_kernel(
    side, scal_ref, blocks_ref, gain_ref, router_ref, lane_ref, other_ref, out_ref,
    win_ref, wout_ref, wide_ref, sems,
):
    core = scal_ref[0]

    @pl.when(core == 0)
    def _():
        pltpu.make_async_copy(lane_ref, win_ref, sems.at[0]).start()
        pltpu.make_async_copy(other_ref, wout_ref, sems.at[1]).start()

    @pl.when(core != 0)
    def _():
        pltpu.make_async_copy(other_ref, win_ref, sems.at[0]).start()
        pltpu.make_async_copy(lane_ref, wout_ref, sems.at[1]).start()

    side.start()
    width = win_ref.shape[1]
    groups = wide_ref.shape[0]
    blocks = load_blocks(blocks_ref, wide_ref)
    parts = [group[:, None] for group in unpack(blocks, 0)[0:3]]
    tall = jnp.concatenate(parts, axis=1).reshape(width, LANES)
    wide = tall.T[0:PACK]
    mean_square = jnp.mean(wide * wide, axis=1, keepdims=True)
    normed = (wide * lax.rsqrt(mean_square + 1e-06) * gain_ref[...]).astype(jnp.bfloat16)
    logit = jnp.sum(normed.astype(jnp.float32) * router_ref[...], axis=1, keepdims=True)
    gate = jax.nn.sigmoid(logit).astype(jnp.bfloat16).astype(jnp.float32)
    pltpu.make_async_copy(lane_ref, win_ref, sems.at[0]).wait()
    pre_act = lax.dot_general(
        normed, win_ref[...], (((1,), (1,)), ((), ())), preferred_element_type=jnp.float32
    )
    side.forward()
    active = jax.nn.gelu(pre_act, approximate=True).astype(jnp.bfloat16)
    pltpu.make_async_copy(lane_ref, wout_ref, sems.at[1]).wait()
    output = jnp.dot(active, wout_ref[...], preferred_element_type=jnp.float32)
    weighted = output * gate
    spread = jnp.broadcast_to(gate, (PACK, LANES))
    zeros = jnp.zeros_like(weighted)
    tall = jnp.concatenate([weighted, zeros], axis=0).T.reshape(groups, 3, 8, LANES)
    gates = jnp.concatenate([spread, jnp.zeros_like(spread)], axis=0).T[0:8]
    gates = jnp.broadcast_to(gates[None], (groups, 8, LANES))
    packed = pack(tall[:, 0], tall[:, 1], tall[:, 2], 0, gates)
    for number in range(groups):
        store_block(out_ref, number, packed[number])
    side.finish()


def run_expert(side, layer, scal, blocks, gains, routers, lane_w, other_w):
    hidden, width = lane_w.shape
    return call_with_side(
        expert_kernel,
        side,
        [scal, blocks, gains, routers, lane_w, other_w],
        [SMEM, VMEM, plane((1, width), layer), plane((1, width), layer), HBM, HBM],
        [jax.ShapeDtypeStruct(blocks.shape, jnp.bfloat16)],
        [VMEM],
        [
            pltpu.VMEM((hidden, width), jnp.bfloat16),
            pltpu.VMEM((hidden, width), jnp.bfloat16),
            pltpu.VMEM((blocks.shape[0] // TILES, 16, LANES), jnp.float32),
            pltpu.SemaphoreType.DMA((2,)),
        ],
        cost_estimate=pl.CostEstimate(
            flops=4 * PACK * hidden * width, bytes_accessed=4 * hidden * width, transcendentals=0
        ),
        name="expert",
    )


def plane(shape, *lead):
    return pl.BlockSpec((None,) * len(lead) + shape, lambda i: lead + (0,) * len(shape))


def place_tokens(routes, experts):
    tokens = routes.shape[2]
    ids = jnp.arange(experts, dtype=jnp.int32)
    first = routes[:, 0, :, None] == ids
    second = routes[:, 1, :, None] == ids
    named = (first | second).astype(jnp.bfloat16)
    earlier = jnp.tril(jnp.ones((tokens, tokens), jnp.bfloat16), -1)
    rank = jnp.einsum("ut,lte->lue", earlier, named, preferred_element_type=jnp.float32)
    rank = rank.astype(jnp.int32) + ids * PACK
    slot_first = jnp.sum(jnp.where(first, rank, 0), axis=2)
    slot_second = jnp.sum(jnp.where(second, rank, 0), axis=2)
    blank = jnp.zeros_like(slot_first)
    return jnp.stack([slot_first, slot_second] + [blank] * 6, axis=1)


def join(*values):
    return lax.optimization_barrier(values)


def local(inputs, routes, norm_gains, routers, expert_in, expert_out):
    sections = lax.axis_size("section")
    experts = lax.axis_size("expert")
    section_pos = lax.axis_index("section")
    repeats, _, _, hidden, width = expert_in.shape
    layers = repeats * sections
    steps, held = ring_plan(sections, layers, PARTS, LEAD)
    size = hidden // PARTS
    scal = jnp.stack([section_pos % 2, section_pos]).astype(jnp.int32)

    buffers = {("in", r): (expert_in, (r, 0, 0)) for r in range(repeats)}
    buffers.update({("out", r): (expert_out, (r, 0, 0)) for r in range(repeats)})
    every = [(lane, y) for lane in range(2) for y in range(sections // 2)]
    table, wanted = [], []

    def source_of(lane, y, i):
        q, part = i // PARTS, i % PARTS
        if q % sections // 2 != y:
            _, number, place = held[lane][y][i]
            return ("ring", number), place * size
        name = ("in", "out")[lane] if q % 2 == lane else "swapped"
        return (name, q // sections), part * size

    def add_pick(by_section):
        choices = sorted(set(by_section.values()))
        table.append([choices.index(by_section.get(s, choices[0])) for s in range(sections)])
        wanted.append(choices)
        return len(table) - 1

    swap_rows = [
        [
            add_pick({2 * y + lane: ((("out", "in")[lane], r), part * size) for lane, y in every})
            for part in range(PARTS)
        ]
        for r in range(repeats)
    ]
    ring_rows = [
        [
            add_pick({2 * y + lane: source_of(lane, y, i) for lane, y, _, i, at in moves if at == place})
            for place in sorted({move[4] for move in moves})
        ]
        for moves in steps
    ]
    layer_rows = [
        [
            add_pick({2 * y + lane: source_of(lane, y, q * PARTS + part) for lane, y in every})
            for part in range(PARTS)
        ]
        for q in range(layers)
    ]
    tab = jnp.asarray(np.array(table, np.int32).T)[section_pos]

    def side_of(tab, *jobs):
        names = sorted({name for rows in jobs for row in rows for name, _ in wanted[row]})
        found = [buffers[name] for name in names]
        plans = [
            tuple(
                (row, tuple((names.index(name), start) for name, start in wanted[row]))
                for row in rows
            )
            for rows in jobs
        ]
        return tab, plans, [array for array, _ in found], [at for _, at in found], size, width

    def picked(rows, tab):
        return pick(side_of(tab, rows))

    def swapped(value):
        return lax.ppermute(value, "section", [(s, s ^ 1) for s in range(sections)])

    def ring(number, value):
        moves = steps[number - 1]
        pairs = sorted({(2 * y + lane, 2 * target + lane) for lane, y, target, _, _ in moves})
        return lax.ppermute(value, "section", pairs)

    def arrival(q):
        parts = range(q * PARTS, (q + 1) * PARTS)
        return max(stock[i][0] for lane in held for stock in lane for i in parts)

    sent = jnp.transpose(routes[:, 0], (1, 0, 3, 2)).astype(jnp.bfloat16).reshape(sections, -1)
    cut = sent.shape[1]
    small = jnp.stack([norm_gains[:, 0], routers[:, 0, 0]]).reshape(1, -1)
    small = jnp.broadcast_to(small, (sections, small.shape[1]))
    sent = jnp.concatenate([sent, small], axis=1).reshape(sections, -1, LANES)
    got = lax.all_to_all(sent, "section", split_axis=0, concat_axis=0, tiled=True)
    h = jnp.transpose(inputs[0], (1, 0))

    ours, later = swapped(picked(swap_rows[0], tab)), swapped(picked(swap_rows[1], tab))
    ours, tab, got = join(ours, tab, got)
    buffers[("swapped", 0)] = (ours, ())
    got = got.reshape(sections, -1)
    mine = got[:, 0:cut].astype(jnp.int32).reshape(sections, repeats, 2, -1)
    mine = jnp.transpose(mine, (1, 0, 2, 3)).reshape(layers, 2, -1)
    rows = place_tokens(mine, experts)
    small = got[:, cut:].reshape(sections, 2, repeats, width)
    small = jnp.transpose(small, (1, 2, 0, 3)).reshape(2, layers, 1, width).astype(jnp.float32)
    gains, gate_rows = small[0], small[1]
    flying = None
    for number in range(1, LEAD + 1):
        started = ring(number, picked(ring_rows[number - 1], tab))
        if number == LEAD:
            h, tab = join(h, tab)
            h, blocks = run_turn(side_of(tab), experts, h, None, rows, None, 0)
            blocks, tab = join(send_blocks(blocks), tab)
        if flying is not None:
            flying, tab = join(flying, tab)
            buffers[("ring", number - 1)] = (flying, ())
        if number == 2:
            later, tab, rows, gains, gate_rows, h = join(later, tab, rows, gains, gate_rows, h)
            buffers[("swapped", 1)] = (later, ())
        flying = started
    flying, tab, blocks = join(flying, tab, blocks)
    buffers[("ring", LEAD)] = (flying, ())
    onward = picked(ring_rows[LEAD], tab)
    flying = ring(LEAD + 1, onward)
    onward, tab = join(onward, tab)
    lane_w = picked(layer_rows[0], tab)
    coming = (lane_w, swapped(lane_w))
    blocks, tab, *coming = join(blocks, tab, *coming)

    for q in range(layers):
        number = LEAD + 1 + q
        if q:
            jobs = ([ring_rows[number - 1]] if number <= len(steps) else []) + (
                [] if coming else [layer_rows[q]]
            )
            h, blocks, *extra = run_turn(side_of(tab, *jobs), experts, h, back, rows, q - 1, q)
            flying = ring(number, extra.pop(0)) if number <= len(steps) else None
            if not coming:
                coming = (extra[0], swapped(extra[0]))
            blocks, tab, *coming = join(send_blocks(blocks), tab, *coming)
        jobs = [layer_rows[q + 1]] if q + 1 < layers and arrival(q + 1) < number else []
        back, *extra = run_expert(
            side_of(tab, *jobs), q, scal, blocks, gains, gate_rows, *coming
        )
        coming = (extra[0], swapped(extra[0])) if jobs else None
        if flying is None:
            back, tab = join(send_blocks(back), tab)
        else:
            back, tab, flying = join(send_blocks(back), tab, flying)
            buffers[("ring", number)] = (flying, ())

    (h,) = run_turn(side_of(tab), experts, h, back, rows, layers - 1, None)
    return jnp.transpose(h, (1, 0))[None]


def solution(mesh):
    return jax.shard_map(
        local,
        mesh=mesh,
        in_specs=(
            P("section", None, "expert"),
            P(None, "section", None, None, None),
            P(None, "section", None),
            P(None, "section", "expert", None),
            P(None, "section", "expert", None, None),
            P(None, "section", "expert", None, None),
        ),
        out_specs=P("section", None, "expert"),
        check_vma=False,
    )
```
